128 devices in a mesh: ctx: 64 (over y, z, x), tp: 2 (over core).
Axes of the slice: x: 4, y: 4, z: 4, core: 2. Of those that a mesh axis runs over, the one named last changes fastest.
Arguments:
- streams: bfloat16 [8192, 3, 8192], P('ctx', None, 'tp'), may hold values from -5 to 5
- short_taps: float32 [7, 3, 8192], P(None, None, 'tp'), may hold values from -1.6 to 1.6
- rates: float32 [16, 8192], P(None, 'tp'), may hold values from 1.2207031e-06 to 0.08
- residues: float32 [16, 8192], P(None, 'tp'), may hold values from -1 to 1
- residual: bfloat16 [8192, 8192], P('ctx', 'tp'), may hold values from -12 to 12
- gain: float32 [8192], P('tp'), may hold values from 0.5 to 1.5
- queries: bfloat16 [8192, 8192], P('ctx', 'tp'), may hold values from -100 to 100
- keys_values: bfloat16 [8192, 2, 1024], P('ctx', None, 'tp'), may hold values from -10 to 10
- lengths: int32 [4], replicated, may hold values from 1 to 4224, 8192 in all
Outputs:
- stream: bfloat16 [8192, 8192], P('ctx', 'tp')
- normed: bfloat16 [8192, 8192], P('ctx', 'tp')
- attended: bfloat16 [8192, 8192], P('ctx', 'tp')
The draws below stay inside these ranges and needn't reach their ends.
Inputs may be any that keep to these rules, and one draw needn't show every extreme that they name: `lengths`: the longest document has exactly 4224 positions.
All inputs are finite; a program needn't handle non-finite values.
Results may differ from the reference program's by a relative error of at most 0.007.
Values may be sent and summed in bfloat16 or wider, within the bound.
No kernel may reach another device: no remote copies, remote signals or barrier semaphores. Data moves between devices by JAX's collectives and lax.ppermute only.
A program may use at most 192 MiB of HBM per device.

```python
import math
import jax
import jax.numpy as jnp
import numpy as np
from jax import lax

D = 8192
HEADS = 64
KV_HEADS = 8
HEAD = 128
MODES = 16
SHORT = 7
SEGS = 4
TOK_DEV = 128
TOKENS = 8192


def key_rows(key):
    return 2.5 * jax.random.truncated_normal(key, -4.0, 4.0, (TOKENS, KV_HEADS * HEAD), jnp.float32)


def draw_keys_values(key, part):
    keys = key_rows(key)
    key = jax.random.fold_in(key, 11)
    values = jax.random.truncated_normal(key, -4.0, 4.0, (TOKENS, KV_HEADS * HEAD), jnp.float32)
    return jnp.stack([keys, values], axis=1).astype(jnp.bfloat16)


def draw_queries(key, part):
    key = jax.random.fold_in(key, 7)
    drawn = jax.random.truncated_normal(key, -4.0, 4.0, (TOKENS, HEADS * HEAD), jnp.float32)
    return drawn.astype(jnp.bfloat16)


def draw_rates(key, part):
    key = jax.random.fold_in(key, 5)
    lowest = jnp.log(0.01 / TOKENS)
    first = jax.random.fold_in(key, 0)
    return jnp.exp(jax.random.uniform(first, (MODES, D), jnp.float32, lowest, jnp.log(0.08))).astype(jnp.float32)


def draw_residual(key, part):
    key = jax.random.fold_in(key, 9)
    columns = jnp.arange(D, dtype=jnp.float32) / D
    drawn = jax.random.truncated_normal(key, -4.0, 4.0, (TOKENS, D), jnp.float32)
    return (drawn * jnp.exp(jnp.log(3.0) * columns)[None, :]).astype(jnp.bfloat16)


def levels(rng, shape, shards, smallest, high):
    factor_of = 1.0
    for dim, shards_of in shards:
        steps = jax.random.uniform(jax.random.fold_in(jax.random.fold_in(rng, 6), dim), (shards_of,), jnp.float32, smallest / len(shards), high / len(shards))
        factor_of = factor_of * jnp.repeat(jnp.exp(steps), shape[dim] // shards_of).reshape((-1,) + (1,) * (len(shape) - 1 - dim))
    return factor_of


def length_profile(amount, total, limit, skew):
    loads = [(1 << 20) // math.isqrt(rank ** skew) + 1 for rank in range(2, amount + 1)]
    rest, given = total - limit - (amount - 1), [1] * (amount - 1)
    while rest > 0:
        candidates = [i for i in range(amount - 1) if given[i] < limit]
        whole, left = sum([loads[i] for i in candidates]), rest
        for i in candidates:
            more = min(limit - given[i], max(1, left * loads[i] // whole), rest)
            given[i] = given[i] + more
            rest = rest - more
    return np.array([limit] + given)


def ragged_sizes(rng, count, total, bound, lean):
    if count == 2:
        one = jax.random.randint(rng, (), max(1, total - bound), min(bound, total - 1) + 1)
        return jnp.stack([one, total - one])
    tallies = jnp.asarray(length_profile(count, total, bound, lean), jnp.int32)
    couples = (count - 1) // 2
    giver, sink = tallies[1:1 + 2 * couples:2], tallies[2:2 + 2 * couples:2]
    margin = jnp.minimum(giver - 1, bound - sink)
    passed = jax.random.randint(jax.random.fold_in(rng, 1), (couples,), 0, 1 << 20) % (margin + 1)
    tallies = tallies.at[1:1 + 2 * couples:2].set(giver - passed).at[2:2 + 2 * couples:2].set(sink + passed)
    return tallies[jax.random.permutation(jax.random.fold_in(rng, 2), count)]


def bell_draw(key, extent, width, reach, cuts=(), kind=jnp.bfloat16):
    values = width * jax.random.normal(key, extent, jnp.float32)
    if cuts:
        values = values * levels(key, extent, cuts, -0.22, 0.18)
    return jnp.clip(values, -reach, reach).astype(kind)


def setup_inputs(seed: int = 0) -> dict:
    seeds = jax.random.split(jax.random.key(seed), 10)
    streams = bell_draw(seeds[0], (TOKENS, 3, D), 1.0, 5.0, ((0, 64), (2, 2)))
    short_taps = bell_draw(seeds[1], (SHORT, 3, D), 0.4, 1.6, ((2, 2),), jnp.float32)
    rates = draw_rates(jax.random.fold_in(seeds[9], 71), 0)
    residues = bell_draw(seeds[3], (MODES, D), 0.25, 1.0, ((1, 2),), jnp.float32)
    residual = draw_residual(jax.random.fold_in(seeds[9], 71), 0)
    gain = jnp.clip(1.0 + 0.1 * jax.random.normal(seeds[5], (D,), jnp.float32), 0.5, 1.5)
    queries = draw_queries(jax.random.fold_in(seeds[9], 71), 0)
    keys_values = draw_keys_values(jax.random.fold_in(seeds[9], 71), 0)
    lengths = ragged_sizes(seeds[8], SEGS, TOKENS, TOKENS // 2 + TOK_DEV, 0).astype(jnp.int32)
    return {"streams": streams, "short_taps": short_taps, "rates": rates, "residues": residues, "residual": residual, "gain": gain, "queries": queries, "keys_values": keys_values, "lengths": lengths}


def document_of(positions, lengths):
    bounds = jnp.cumsum(lengths).astype(jnp.int32)
    return lax.optimization_barrier(jnp.sum((positions[:, None] >= bounds[None, :]).astype(jnp.int32), axis=1))

def reference(streams, short_taps, rates, residues, residual, gain, queries, keys_values, lengths):
    group = HEADS // KV_HEADS
    positions = jnp.arange(TOKENS, dtype=jnp.int32)
    documents = document_of(positions, lengths)
    keys = keys_values[:, 0].astype(jnp.float32).reshape(TOKENS, KV_HEADS, HEAD)
    values = keys_values[:, 1].astype(jnp.float32).reshape(TOKENS, KV_HEADS, HEAD)
    block = 128
    count = TOKENS // block
    query_blocks = queries.reshape(count, block, KV_HEADS, group, HEAD)

    def attend(item):
        query_block, index = item
        query_pos = index * block + jnp.arange(block, dtype=jnp.int32)
        query_doc = document_of(query_pos, lengths)
        scores = jnp.einsum('tkgd,skd->tkgs', query_block.astype(jnp.float32), keys) / jnp.sqrt(jnp.float32(HEAD))
        allowed = (positions[None, :] <= query_pos[:, None]) & (documents[None, :] == query_doc[:, None])
        allowed = allowed[:, None, None, :]
        masked = jnp.where(allowed, scores, jnp.float32(-1e+30))
        top = lax.optimization_barrier(jnp.max(masked, axis=-1, keepdims=True))
        weights = jnp.where(allowed, jnp.exp(masked - top), jnp.float32(0.0))
        totals = lax.optimization_barrier(jnp.sum(weights, axis=-1))
        rounded = lax.optimization_barrier(weights.astype(jnp.bfloat16)).astype(jnp.float32)
        mixed = jnp.einsum('tkgs,skd->tkgd', rounded, values) / totals[..., None]
        return mixed.astype(jnp.bfloat16).reshape(block, HEADS * HEAD)
    attended = lax.map(attend, (query_blocks, jnp.arange(count, dtype=jnp.int32))).reshape(TOKENS, HEADS * HEAD)
    inputs = streams.astype(jnp.float32)
    padded = jnp.concatenate([jnp.zeros((SHORT - 1, 3, D), jnp.float32), inputs], axis=0)
    filtered = jnp.zeros_like(inputs)
    for offset in range(SHORT):
        filtered = filtered + short_taps[offset] * padded[SHORT - 1 - offset:SHORT - 1 - offset + TOKENS]
    gated = filtered[:, 1] * filtered[:, 2]
    decay = jnp.exp(-rates)
    mode_weight = residues * jnp.sqrt(-jnp.expm1(-2.0 * rates))

    def advance(state, column):
        state = decay * state + column[None, :]
        return (state, lax.optimization_barrier(jnp.sum(mode_weight * state, axis=0)))
    unused, long_out = lax.scan(advance, jnp.zeros((MODES, D), jnp.float32), gated)
    stream = (residual.astype(jnp.float32) + attended.astype(jnp.float32) + filtered[:, 0] * long_out).astype(jnp.bfloat16)
    wide = stream.astype(jnp.float32)
    mean_square = lax.optimization_barrier(jnp.mean(wide * wide, axis=1, keepdims=True))
    normed = (wide * lax.rsqrt(mean_square + 1e-06) * gain).astype(jnp.bfloat16)
    return (stream, normed, attended)
```

```python
import math

import jax
import jax.numpy as jnp
from jax import lax
from jax.experimental import pallas as pl
from jax.experimental.pallas import tpu as pltpu
from jax.sharding import Mesh
from jax.sharding import PartitionSpec as P

HEAD = 128
SHORT = 7
MODES = 16
ROWS = 128
SIDE = 4
LANES = 128
SUB = 8
GROUP = SUB * LANES
CHUNK = SIDE * ROWS
SCALE = math.log2(math.e) / math.sqrt(HEAD)
NEG = -1e30


def turn(value, axis, distance):
    if distance % SIDE == 0:
        return value
    return lax.ppermute(value, axis, [(i, (i + distance) % SIDE) for i in range(SIDE)])


def mixer_kernel(x_ref, halo_ref, taps_ref, decay_ref, weight_ref, residual_ref,
                 base_ref, first_ref, end_ref, window, gated, out):
    def filtered(j):
        window[0:SUB] = halo_ref[j]
        window[SUB:] = x_ref[j].astype(jnp.float32)
        total = taps_ref[j, 0:1] * window[SUB:SUB + ROWS]
        for i in range(1, SHORT):
            total = total + taps_ref[j, i:i + 1] * window[SUB - i:SUB - i + ROWS]
        return total

    first_ref[...] = filtered(1)
    product = first_ref[...] * filtered(2)
    for c in range(SUB):
        gated[pl.ds(c, ROWS, stride=SUB), :] = product[:, c * LANES:(c + 1) * LANES]
    first_ref[...] = filtered(0)

    def step(t, states):
        rows = pl.ds(pl.multiple_of(t * SUB, SUB), SUB)
        g = gated[rows, :]
        fresh = tuple(decay_ref[n] * states[n] + g for n in range(MODES))
        parts = [weight_ref[n] * fresh[n] for n in range(MODES)]
        while len(parts) > 1:
            parts = [a + b for a, b in zip(parts[::2], parts[1::2])]
        out[rows, :] = parts[0]
        return fresh

    zero = jnp.zeros((SUB, LANES), jnp.float32)
    states = lax.fori_loop(0, ROWS, step, (zero,) * MODES)
    for n in range(MODES):
        end_ref[n] = states[n]
    for c in range(SUB):
        cols = slice(c * LANES, (c + 1) * LANES)
        base_ref[:, cols] = (
            residual_ref[:, cols].astype(jnp.float32)
            + first_ref[:, cols] * out[pl.ds(c, ROWS, stride=SUB), :]
        )


def carried_kernel(state_ref, decay_ref, weight_ref, base_ref, first_ref, full_ref, out):
    def step(t, states):
        rows = pl.ds(pl.multiple_of(t * SUB, SUB), SUB)
        fresh = tuple(decay_ref[n] * states[n] for n in range(MODES))
        parts = list(fresh)
        while len(parts) > 1:
            parts = [a + b for a, b in zip(parts[::2], parts[1::2])]
        out[rows, :] = parts[0]
        return fresh

    lax.fori_loop(0, ROWS, step, tuple(weight_ref[n] * state_ref[n] for n in range(MODES)))
    for c in range(SUB):
        cols = slice(c * LANES, (c + 1) * LANES)
        full_ref[:, cols] = base_ref[:, cols] + first_ref[:, cols] * out[pl.ds(c, ROWS, stride=SUB), :]


def attend_kernel(place_ref, lengths_ref, q_ref, a0, a1, a2, a3, b0, b1, b2, b3, o_ref,
                  q_rows, keys, values, accum, largest, sems):
    y, z, x, back = place_ref[0], place_ref[1], place_ref[2], place_ref[3]
    query_block = 16 * lax.rem(y - back + SIDE, SIDE) + 4 * z + x
    query_first = query_block * ROWS
    bounds = []
    total = 0
    for i in range(4):
        total = total + lengths_ref[i]
        bounds.append(total)

    def document_start(position):
        start = jnp.zeros_like(position)
        for bound in bounds:
            start = jnp.maximum(start, jnp.where(position >= bound, bound, 0))
        return start

    first_start = document_start(query_first)
    last_start = document_start(query_first + ROWS - 1)
    top = query_block // SIDE
    low = first_start // CHUNK
    halves = ((a0, a1, a2, a3), (b0, b1, b2, b3))

    def copies(chunk, slot, act):
        plane, row = chunk // SIDE, lax.rem(chunk, SIDE)
        turned = lax.rem(y - plane + SIDE, SIDE)
        behind = lax.rem(z - row + SIDE, SIDE)

        def pair(source, k):
            target = lax.rem(x - k + SIDE, SIDE)
            rows = pl.ds(pl.multiple_of(target * ROWS, ROWS), ROWS)
            act(pltpu.make_async_copy(source.at[0], keys.at[slot, rows], sems.at[slot, k]))
            act(pltpu.make_async_copy(source.at[1], values.at[slot, rows, pl.ds(0, HEAD)], sems.at[slot, 4 + k]))

        for m in range(SIDE):
            @pl.when((turned < 2) & (behind == m))
            def _():
                for k in range(SIDE):
                    pair(halves[0][m].at[k, turned], k)

        @pl.when(turned >= 2)
        def _():
            for m in range(SIDE):
                pair(halves[1][m].at[behind, turned - 2], m)

    copies(top, 0, lambda c: c.start())
    for g in range(SUB):
        q_rows[g * ROWS:(g + 1) * ROWS] = q_ref[:, g * HEAD:(g + 1) * HEAD]
    values[:, :, HEAD:] = jnp.ones((2, CHUNK, HEAD), jnp.bfloat16)
    accum[...] = jnp.zeros_like(accum)
    largest[...] = jnp.full_like(largest, NEG)

    def one(step, carry):
        chunk = top - step
        slot = lax.rem(step, 2)

        @pl.when(chunk > low)
        def _():
            copies(chunk - 1, 1 - slot, lambda c: c.start())

        copies(chunk, slot, lambda c: c.wait())
        key_first = chunk * CHUNK
        whole = (key_first + CHUNK - 1 <= query_first) & (key_first >= last_start)

        def update(masked):
            scores = lax.dot_general(
                q_rows[...], keys[slot], (((1,), (1,)), ((), ())), preferred_element_type=jnp.float32
            )
            if masked:
                query_pos = query_first + lax.broadcasted_iota(jnp.int32, (ROWS, CHUNK), 0)
                key_pos = key_first + lax.broadcasted_iota(jnp.int32, (ROWS, CHUNK), 1)
                allowed = (key_pos <= query_pos) & (key_pos >= document_start(query_pos))
                bias = jnp.where(allowed, 0.0, NEG)
                scores = (scores.reshape(SUB, ROWS, CHUNK) + bias[None]).reshape(SUB * ROWS, CHUNK)
            before = largest[...]
            fresh = jnp.maximum(before, SCALE * jnp.max(scores, axis=1, keepdims=True))
            weights = jnp.exp2(scores * SCALE - fresh[:, 0:1]).astype(jnp.bfloat16)
            added = jnp.dot(weights, values[slot], preferred_element_type=jnp.float32)
            shrink = jnp.exp2(before - fresh)
            largest[...] = fresh
            accum[:, :HEAD] = accum[:, :HEAD] * shrink + added[:, :HEAD]
            accum[:, HEAD:] = accum[:, HEAD:] * shrink + added[:, HEAD:]

        pl.when(whole)(lambda: update(False))
        pl.when(jnp.logical_not(whole))(lambda: update(True))
        return carry

    lax.fori_loop(0, top - low + 1, one, 0)
    for g in range(SUB):
        rows = slice(g * ROWS, (g + 1) * ROWS)
        o_ref[:, g * HEAD:(g + 1) * HEAD] = (accum[rows, :HEAD] / accum[rows, HEAD:]).astype(jnp.bfloat16)


def mixer(x, halo, taps, decay, weight, residual):
    width = residual.shape[1]
    steps = width // GROUP
    flat = jax.ShapeDtypeStruct((ROWS, width), jnp.float32)
    return pl.pallas_call(
        mixer_kernel,
        grid=(steps,),
        in_specs=[
            pl.BlockSpec((3, ROWS, GROUP), lambda i: (0, 0, i)),
            pl.BlockSpec((3, SUB, GROUP), lambda i: (0, 0, i)),
            pl.BlockSpec((3, SHORT, GROUP), lambda i: (0, 0, i)),
            pl.BlockSpec((MODES, SUB, LANES), lambda i: (0, i, 0)),
            pl.BlockSpec((MODES, SUB, LANES), lambda i: (0, i, 0)),
            pl.BlockSpec((ROWS, GROUP), lambda i: (0, i)),
        ],
        out_specs=[
            pl.BlockSpec((ROWS, GROUP), lambda i: (0, i)),
            pl.BlockSpec((ROWS, GROUP), lambda i: (0, i)),
            pl.BlockSpec((MODES, SUB, LANES), lambda i: (0, i, 0)),
        ],
        out_shape=[flat, flat, jax.ShapeDtypeStruct(decay.shape, jnp.float32)],
        scratch_shapes=[
            pltpu.VMEM((SUB + ROWS, GROUP), jnp.float32),
            pltpu.VMEM((ROWS * SUB, LANES), jnp.float32),
            pltpu.VMEM((ROWS * SUB, LANES), jnp.float32),
        ],
        compiler_params=pltpu.CompilerParams(vmem_limit_bytes=32 * 1024 * 1024),
        cost_estimate=pl.CostEstimate(flops=80_000_000, bytes_accessed=10_000_000, transcendentals=0),
        name="mixer",
    )(x, halo, taps, decay, weight, residual)


def carried(state, decay, weight, base, first):
    width = base.shape[1]
    steps = width // GROUP
    modes = pl.BlockSpec((MODES, SUB, LANES), lambda i: (0, i, 0))
    rows = pl.BlockSpec((ROWS, GROUP), lambda i: (0, i))
    return pl.pallas_call(
        carried_kernel,
        grid=(steps,),
        in_specs=[modes, modes, modes, rows, rows],
        out_specs=rows,
        out_shape=jax.ShapeDtypeStruct((ROWS, width), jnp.float32),
        scratch_shapes=[pltpu.VMEM((ROWS * SUB, LANES), jnp.float32)],
        compiler_params=pltpu.CompilerParams(vmem_limit_bytes=32 * 1024 * 1024),
        cost_estimate=pl.CostEstimate(flops=20_000_000, bytes_accessed=6_000_000, transcendentals=0),
        name="carried",
    )(state, decay, weight, base, first)


def attend(place, lengths, q, blocks):
    smem = pl.BlockSpec(memory_space=pltpu.SMEM)
    vmem = pl.BlockSpec(memory_space=pltpu.VMEM)
    return pl.pallas_call(
        attend_kernel,
        in_specs=[smem, smem, vmem] + [pl.BlockSpec(memory_space=pl.ANY)] * 8,
        out_specs=vmem,
        out_shape=jax.ShapeDtypeStruct(q.shape, jnp.bfloat16),
        scratch_shapes=[
            pltpu.VMEM((SUB * ROWS, HEAD), jnp.bfloat16),
            pltpu.VMEM((2, CHUNK, HEAD), jnp.bfloat16),
            pltpu.VMEM((2, CHUNK, 2 * HEAD), jnp.bfloat16),
            pltpu.VMEM((SUB * ROWS, 2 * HEAD), jnp.float32),
            pltpu.VMEM((SUB * ROWS, LANES), jnp.float32),
            pltpu.SemaphoreType.DMA((2, 8)),
        ],
        compiler_params=pltpu.CompilerParams(vmem_limit_bytes=40 * 1024 * 1024),
        cost_estimate=pl.CostEstimate(flops=3_000_000_000, bytes_accessed=2_000_000, transcendentals=3_000_000),
        name="attend",
    )(place, lengths, q, *blocks)


def local(streams, short_taps, rates, residues, residual, gain, queries, keys_values, lengths):
    width = residual.shape[1]
    head_cols = width // SIDE
    y, z, x = (lax.axis_index(a) for a in ("y", "z", "x"))
    ctx = ("y", "z", "x")

    by_head = keys_values.reshape(ROWS, 2, SIDE, HEAD).transpose(2, 1, 0, 3)
    near = [
        turn(lax.dynamic_index_in_dim(by_head, lax.rem(y + r, SIDE), 0, False), "y", r) for r in range(SIDE)
    ]
    part_a, part_b = jnp.stack(near[:2]), jnp.stack(near[2:])
    row_a = jnp.stack([turn(part_a, "x", k) for k in range(SIDE)])
    row_b = jnp.stack([turn(part_b, "z", k) for k in range(SIDE)])
    blocks = [turn(row_a, "z", m) for m in range(SIDE)] + [turn(row_b, "x", m) for m in range(SIDE)]

    asked = [
        turn(lax.dynamic_slice_in_dim(queries, lax.rem(y + r, SIDE) * head_cols, head_cols, 1), "y", r)
        for r in range(SIDE)
    ]

    by_stream = streams.transpose(1, 0, 2)
    route = [(i, i + 1) for i in range(SIDE**3 - 1)]
    halo = lax.ppermute(by_stream[:, ROWS - SUB:], ctx, route).astype(jnp.float32)
    rate = rates.reshape(MODES, width // LANES, LANES)
    decay = jnp.exp(-rate)
    weight = residues.reshape(MODES, width // LANES, LANES) * jnp.sqrt(-jnp.expm1(-2.0 * rate))
    base, first, end = mixer(by_stream, halo, short_taps.transpose(1, 0, 2), decay, weight, residual)

    def level(value, axis, place, span, last):
        sent = value.astype(jnp.bfloat16)
        others = [turn(sent, axis, k).astype(jnp.float32) for k in range(1, SIDE)]
        before = jnp.zeros_like(value)
        total = value * jnp.exp(-rate * (span * (SIDE - 1 - place)).astype(jnp.float32))
        for k, other in enumerate(others, 1):
            kept = jnp.exp(-rate * float(span * (k - 1)))
            before = before + jnp.where(place >= k, kept * other, 0.0)
            origin = lax.rem(place - k + SIDE, SIDE)
            total = total + other * jnp.exp(-rate * (span * (SIDE - 1 - origin)).astype(jnp.float32))
        return before, total

    before_x, total_x = level(end, "x", x, ROWS, False)
    before_z, total_z = level(total_x, "z", z, ROWS * SIDE, False)
    before_y, _ = level(total_z, "y", y, ROWS * SIDE * SIDE, True)
    entering = (
        before_x
        + jnp.exp(-rate * (ROWS * x).astype(jnp.float32)) * before_z
        + jnp.exp(-rate * (ROWS * (SIDE * z + x)).astype(jnp.float32)) * before_y
    )
    base = carried(entering, decay, weight, base, first)

    parts = {}
    for r in (2, 1, 3, 0):
        place = jnp.stack([y, z, x, jnp.int32(r)])
        parts[r] = turn(attend(place, lengths, asked[r], blocks), "y", SIDE - r)
    attended = jnp.zeros(residual.shape, jnp.bfloat16)
    for r in range(SIDE):
        attended = lax.dynamic_update_slice_in_dim(attended, parts[r], lax.rem(y + r, SIDE) * head_cols, 1)

    stream = (base + attended.astype(jnp.float32)).astype(jnp.bfloat16)
    wide = stream.astype(jnp.float32)
    squares = lax.psum(jnp.sum(wide * wide, axis=1), "tp")
    mean_square = squares / (width * lax.axis_size("tp"))
    normed = (wide * lax.rsqrt(mean_square[:, None] + 1e-06) * gain).astype(jnp.bfloat16)
    return (stream, normed, attended)


def solution(mesh):
    split = Mesh(mesh.devices.reshape(SIDE, SIDE, SIDE, 2), ("y", "z", "x", "tp"))
    ctx = ("y", "z", "x")
    in_specs = (
        P(ctx, None, "tp"),
        P(None, None, "tp"),
        P(None, "tp"),
        P(None, "tp"),
        P(ctx, "tp"),
        P("tp"),
        P(ctx, "tp"),
        P(ctx, None, "tp"),
        P(),
    )
    out_specs = (P(ctx, "tp"), P(ctx, "tp"), P(ctx, "tp"))
    return jax.shard_map(local, mesh=split, in_specs=in_specs, out_specs=out_specs, check_vma=False)
```

```python
import math

import jax
import jax.numpy as jnp
from jax import lax
from jax.experimental import pallas as pl
from jax.experimental.pallas import tpu as pltpu
from jax.sharding import Mesh
from jax.sharding import PartitionSpec as P

HEAD = 128
SHORT = 7
MODES = 16
ROWS = 128
SIDE = 4
LANES = 128
SUB = 8
GROUP = SUB * LANES
CHUNK = SIDE * ROWS
SCALE = math.log2(math.e) / math.sqrt(HEAD)
NEG = -1e30
SAFE = 100.0
MESH = ("y", "z", "x", "tp")
VMEM = pl.BlockSpec(memory_space=pltpu.VMEM)
SMEM = pl.BlockSpec(memory_space=pltpu.SMEM)
ANY = pl.BlockSpec(memory_space=pl.ANY)
PARAMS = pltpu.CompilerParams(vmem_limit_bytes=40 * 1024 * 1024)


def spread(moves):
    route = []
    for i in range(2 * SIDE**3):
        y, z, x, core = i // 32, i // 8 % SIDE, i // 2 % SIDE, i % 2
        dy, dz, dx = moves(core)
        y, z, x = (y + dy) % SIDE, (z + dz) % SIDE, (x + dx) % SIDE
        route.append((i, y * 32 + z * 8 + x * 2 + core))
    return route


def turn(value, axis, distance):
    if distance % SIDE == 0:
        return value
    return lax.ppermute(value, axis, [(i, (i + distance) % SIDE) for i in range(SIDE)])


def turn_cores(value, distance, axes):
    if distance == 0:
        return value
    return lax.ppermute(value, MESH, spread(lambda core: tuple(distance * (a == axes[core]) for a in "yzx")))


def apart_kernel(place_ref, kv_ref, *out_refs):
    for r, out_ref in enumerate(out_refs):
        head = (place_ref[0] + r) & (SIDE - 1)
        cols = pl.ds(pl.multiple_of(head * HEAD, HEAD), HEAD)
        for j in range(2):
            out_ref[j] = kv_ref[:, j, cols]


def mixer_kernel(x_ref, halo_ref, taps_ref, rates_ref, weights_ref, residual_ref,
                 base_ref, first_ref, end_ref, rate_ref, weight_ref,
                 window, taps, modes, gated, out):
    for c in range(SUB):
        cols = slice(c * LANES, (c + 1) * LANES)
        for j in range(3):
            window[j, pl.ds(c, SUB, stride=SUB), :] = halo_ref[j, :, cols].astype(jnp.float32)
            window[j, pl.ds(SUB * SUB + c, ROWS, stride=SUB), :] = x_ref[j, :, cols].astype(jnp.float32)
            taps[j, pl.ds(c, SHORT, stride=SUB), :] = taps_ref[j, :, cols]
        modes[0, pl.ds(c, MODES, stride=SUB), :] = rates_ref[:, cols]
        modes[1, pl.ds(c, MODES, stride=SUB), :] = weights_ref[:, cols]
    for n in range(MODES):
        rate_ref[n] = modes[0, n * SUB:(n + 1) * SUB]
        weight_ref[n] = modes[1, n * SUB:(n + 1) * SUB]
    modes[0] = jnp.exp(-modes[0])

    def short(i, unused):
        start = i * (SUB * SUB)
        found = []
        for j in range(3):
            tap = [taps[j, k * SUB:(k + 1) * SUB] for k in range(SHORT)]
            seen = [
                window[j, pl.ds(pl.multiple_of(start + (SUB - SHORT + 1 + k) * SUB, SUB), SUB), :]
                for k in range(SUB + SHORT - 1)
            ]
            sums = []
            for u in range(SUB):
                total = tap[0] * seen[SHORT - 1 + u]
                for k in range(1, SHORT):
                    total = total + tap[k] * seen[SHORT - 1 + u - k]
                sums.append(total)
            found.append(sums)
        for u in range(SUB):
            rows = pl.ds(pl.multiple_of(start + u * SUB, SUB), SUB)
            first_ref[rows, :] = found[0][u]
            gated[rows, :] = found[1][u] * found[2][u]
        return unused

    lax.fori_loop(0, ROWS // SUB, short, 0)

    def step(t, states):
        rows = pl.ds(pl.multiple_of(t * SUB, SUB), SUB)
        g = gated[rows, :]
        fresh, sums = [], [None, None]
        for n in range(MODES):
            state = modes[0, n * SUB:(n + 1) * SUB] * states[n] + g
            fresh.append(state)
            part = modes[1, n * SUB:(n + 1) * SUB] * state
            sums[n % 2] = part if sums[n % 2] is None else sums[n % 2] + part
        out[rows, :] = (sums[0] + sums[1]) * first_ref[rows, :]
        return tuple(fresh)

    zero = jnp.zeros((SUB, LANES), jnp.float32)
    states = lax.fori_loop(0, ROWS, step, (zero,) * MODES, unroll=4)
    for n in range(MODES):
        end_ref[n] = states[n]
    for c in range(SUB):
        cols = slice(c * LANES, (c + 1) * LANES)
        base_ref[:, cols] = residual_ref[:, cols].astype(jnp.float32) + out[pl.ds(c, ROWS, stride=SUB), :]


def carried_kernel(state_ref, rate_ref, weight_ref, base_ref, first_ref, after_ref, full_ref, decay, out):
    decay[...] = jnp.exp(-rate_ref[...])

    def step(t, states):
        rows = pl.ds(pl.multiple_of(t * SUB, SUB), SUB)
        fresh, sums = [], [None, None]
        for n in range(MODES):
            state = decay[n] * states[n]
            fresh.append(state)
            sums[n % 2] = state if sums[n % 2] is None else sums[n % 2] + state
        out[rows, :] = (sums[0] + sums[1]) * first_ref[rows, :]
        return tuple(fresh)

    lax.fori_loop(0, ROWS, step, tuple(weight_ref[n] * state_ref[n] for n in range(MODES)), unroll=4)
    for c in range(SUB):
        cols = slice(c * LANES, (c + 1) * LANES)
        full_ref[:, cols] = base_ref[:, cols] + out[pl.ds(c, ROWS, stride=SUB), :]


def level_kernel(span, which, place_ref, rate_ref, own_ref, one_ref, two_ref, three_ref, after_ref, before_ref, total_ref):
    place = place_ref[which]

    def one(n, unused):
        rate = rate_ref[n] * float(span)
        total = own_ref[n] * jnp.exp(-rate * (SIDE - 1 - place).astype(jnp.float32))
        before = jnp.zeros_like(total)
        for k, ref in enumerate((one_ref, two_ref, three_ref), 1):
            other = ref[n].astype(jnp.float32)
            origin = (place - k) & (SIDE - 1)
            total = total + other * jnp.exp(-rate * (SIDE - 1 - origin).astype(jnp.float32))
            kept = other if k == 1 else other * jnp.exp(-rate * float(k - 1))
            before = before + kept * jnp.where(place >= k, 1.0, 0.0)
        before_ref[n] = before
        total_ref[n] = total
        return unused

    lax.fori_loop(0, MODES, one, 0)


def entering_kernel(place_ref, rate_ref, x_ref, z_ref, one_ref, two_ref, three_ref, after_ref, state_ref):
    y, z, x = place_ref[0], place_ref[1], place_ref[2]

    def one(n, unused):
        rate = rate_ref[n] * float(ROWS)
        before = jnp.zeros_like(rate)
        for k, ref in enumerate((one_ref, two_ref, three_ref), 1):
            kept = ref[n].astype(jnp.float32) * jnp.exp(-rate * float(SIDE * SIDE * (k - 1)))
            before = before + kept * jnp.where(y >= k, 1.0, 0.0)
        state_ref[n] = (
            x_ref[n]
            + jnp.exp(-rate * x.astype(jnp.float32)) * z_ref[n]
            + jnp.exp(-rate * (SIDE * z + x).astype(jnp.float32)) * before
        )
        return unused

    lax.fori_loop(0, MODES, one, 0)


def attend_kernel(backs, near, place_ref, lengths_ref, *refs):
    count = len(backs)
    refs = list(refs)
    q_refs = [refs.pop(0) for _ in backs]
    pieces = [refs.pop(0) for _ in range(1 if near else SIDE - 1)]
    if near:
        refs.pop(0)
        sums_ref, shift_ref = refs.pop(0), refs.pop(0)
    else:
        sums_in, shift_in = refs.pop(0), refs.pop(0)
        refs.pop(0)
        refs.pop(0)
        o_refs = [refs.pop(0) for _ in backs]
    q_rows, keys, values, accum, largest = refs
    y, z, x, core = place_ref[0], place_ref[1], place_ref[2], place_ref[3]
    bounds = []
    total = 0
    for i in range(4):
        total = total + lengths_ref[i]
        bounds.append(total)

    def document_start(position):
        start = jnp.zeros_like(position)
        for bound in bounds:
            start = jnp.maximum(start, jnp.where(position >= bound, bound, 0))
        return start

    values[:, HEAD:] = jnp.ones((CHUNK, HEAD), jnp.bfloat16)

    def query(s, unused):
        back = jnp.int32(backs[0])
        for i in range(1, count):
            back = jnp.where(s == i, backs[i], back)
        query_block = 16 * ((y - back) & (SIDE - 1)) + SIDE * z + x
        query_first = query_block * ROWS
        last_start = document_start(query_first + ROWS - 1)
        low = document_start(query_first) // ROWS

        plane, row = query_block >> 4, query_block >> 2

        def near_below(block):
            by_row = 4 * (block >> 4) + jnp.clip((block & 15) - 4 * z, 0, SIDE)
            return jnp.where(core == 0, by_row, (block + 3 - x) >> 2)

        found = near_below(query_block + 1) - near_below(low)
        if not near:
            found = query_block - low + 1 - found

        def block_of(i):
            if near:
                here = jnp.where(core == 0, x, z)
                j = i - here - 1
                below, left = 16 * (plane - 1 - (j >> 2)), 3 - (j & 3)
                mine = query_block - jnp.where(core == 0, i, 4 * i)
                other = below + jnp.where(core == 0, 4 * z + left, 4 * left + x)
                block = jnp.where(i <= here, mine, other)
            else:
                j = (i >> 2) - z
                left = 3 - lax.rem(j, 3)
                left = left - jnp.where(left <= z, 1, 0)
                above = 4 * (4 * (plane - 1 - j // 3) + left)
                by_row = jnp.where(j < 0, 16 * plane + 4 * (z - 1 - (i >> 2)), above) + 3 - (i & 3)
                k = i - x
                left = 3 - lax.rem(k, 3)
                left = left - jnp.where(left <= x, 1, 0)
                by_column = jnp.where(k < 0, query_block - 1 - i, 4 * (row - 1 - k // 3) + left)
                block = jnp.where(core == 0, by_row, by_column)
            return jnp.where(i < found, block, -1)

        chunks = (found + SIDE - 1) // SIDE

        def fetch(chunk):
            for i in range(SIDE):
                block = jnp.maximum(block_of(chunk * SIDE + i), 0)
                turned = (y - (block >> 4)) & (SIDE - 1)
                behind_z = (z - (block >> 2)) & (SIDE - 1)
                behind_x = (x - block) & (SIDE - 1)
                outer = jnp.where(core == 0, behind_z, behind_x)
                inner = jnp.where(core == 0, behind_x, behind_z)
                rows = slice(i * ROWS, (i + 1) * ROWS)

                def pair(source):
                    keys[rows] = source[inner, turned, 0]
                    values[rows, :HEAD] = source[inner, turned, 1]

                if near:
                    pair(pieces[0])
                else:
                    pl.when(outer <= 1)(lambda: pair(pieces[0]))
                    pl.when(outer == 2)(lambda: pair(pieces[1]))
                    pl.when(outer == 3)(lambda: pair(pieces[2]))

        for i in range(count):
            @pl.when(s == i)
            def _():
                for g in range(SUB):
                    q_rows[g * ROWS:(g + 1) * ROWS] = q_refs[i][:, g * HEAD:(g + 1) * HEAD]

        if near:
            accum[...] = jnp.zeros_like(accum)
        else:
            accum[...] = sums_in[back]
            largest[...] = shift_in[back]

        def scored():
            return lax.dot_general(
                q_rows[...], keys[...], (((1,), (1,)), ((), ())), preferred_element_type=jnp.float32
            )

        def masked(scores, chunk):
            query_pos = query_first + lax.broadcasted_iota(jnp.int32, (ROWS, ROWS), 0)
            start = document_start(query_pos)
            lane = lax.broadcasted_iota(jnp.int32, (ROWS, ROWS), 1)
            parts = []
            for i in range(SIDE):
                key_pos = block_of(chunk * SIDE + i) * ROWS + lane
                parts.append(jnp.where((key_pos <= query_pos) & (key_pos >= start), 0.0, NEG))
            bias = jnp.concatenate(parts, axis=1)
            return (scores.reshape(SUB, ROWS, CHUNK) + bias[None]).reshape(SUB * ROWS, CHUNK)

        def weighed(scores, shift):
            parts = [scores[:, i * LANES:(i + 1) * LANES] * SCALE - shift for i in range(SIDE)]
            weights = jnp.concatenate([jnp.exp2(p).astype(jnp.bfloat16) for p in parts], axis=1)
            high = jnp.maximum(jnp.maximum(parts[0], parts[1]), jnp.maximum(parts[2], parts[3]))
            return jnp.dot(weights, values[...], preferred_element_type=jnp.float32), high

        def one(chunk, carry):
            fetch(chunk)
            if near:
                @pl.when(chunk == 0)
                def _():
                    own = keys[0:ROWS].astype(jnp.float32) * SCALE
                    paired = q_rows[...].astype(jnp.float32).reshape(SUB, ROWS, HEAD) * own[None]
                    largest[...] = jnp.dot(
                        paired.reshape(SUB * ROWS, HEAD).astype(jnp.bfloat16),
                        jnp.ones((HEAD, LANES), jnp.bfloat16),
                        preferred_element_type=jnp.float32,
                    )

            def update(scores):
                added, high = weighed(scores, largest[...])
                high = jnp.max(high.reshape(ROWS, SUB, LANES), axis=0)
                fits = jnp.max(high) < SAFE

                @pl.when(fits)
                def _():
                    accum[...] += added

                @pl.when(jnp.logical_not(fits))
                def _():
                    scores = masked(scored(), chunk)
                    before = largest[...]
                    fresh = jnp.maximum(before, SCALE * jnp.max(scores, axis=1, keepdims=True))
                    shrink = jnp.exp2(before - fresh)
                    largest[...] = fresh
                    added = weighed(scores, fresh)[0]
                    accum[...] = accum[...] * jnp.concatenate([shrink, shrink], axis=1) + added

            whole = (block_of(chunk * SIDE) < query_block) & (block_of(chunk * SIDE + SIDE - 1) * ROWS >= last_start)
            pl.when(whole)(lambda: update(scored()))
            pl.when(jnp.logical_not(whole))(lambda: update(masked(scored(), chunk)))
            return carry

        lax.fori_loop(0, chunks, one, 0)
        if near:
            sums_ref[back] = accum[...]
            shift_ref[back] = largest[...]
        else:
            for i in range(count):
                @pl.when(s == i)
                def _():
                    for g in range(SUB):
                        rows = slice(g * ROWS, (g + 1) * ROWS)
                        o_refs[i][:, g * HEAD:(g + 1) * HEAD] = (
                            accum[rows, :HEAD] / accum[rows, HEAD:]
                        ).astype(jnp.bfloat16)
        return unused

    lax.fori_loop(0, count, query, 0)


def joined(place_ref, base_ref, parts, store):
    rows, width = base_ref.shape
    cols = width // SIDE
    for r, part in enumerate(parts):
        start = pl.multiple_of(((place_ref[0] + r) & (SIDE - 1)) * cols, cols)
        heads = part[...]
        stream = base_ref[:, pl.ds(start, cols)] + heads.astype(jnp.float32)
        store(pl.ds(start, cols), heads, stream.astype(jnp.bfloat16))


def squares_kernel(place_ref, base_ref, p0, p1, p2, p3, squares_ref):
    squares_ref[...] = jnp.zeros_like(squares_ref)

    def store(cols, heads, stream):
        wide = stream.astype(jnp.float32)
        squares_ref[...] += jnp.sum(wide * wide, axis=1, keepdims=True)

    joined(place_ref, base_ref, (p0, p1, p2, p3), store)


def stream_kernel(place_ref, base_ref, p0, p1, p2, p3, squares_ref, stream_ref, attended_ref):
    def store(cols, heads, stream):
        attended_ref[:, cols] = heads
        stream_ref[:, cols] = stream

    joined(place_ref, base_ref, (p0, p1, p2, p3), store)


def normed_kernel(width, stream_ref, gain_ref, own_ref, other_ref, normed_ref):
    factor = lax.rsqrt((own_ref[...] + other_ref[...]) / (2 * width) + 1e-06)
    normed_ref[...] = (stream_ref[...].astype(jnp.float32) * factor * gain_ref[...]).astype(jnp.bfloat16)


def apart(place, keys_values):
    return pl.pallas_call(
        apart_kernel,
        in_specs=[SMEM, VMEM],
        out_specs=[VMEM] * SIDE,
        out_shape=[jax.ShapeDtypeStruct((2, ROWS, HEAD), jnp.bfloat16)] * SIDE,
        compiler_params=PARAMS,
        name="apart",
    )(place, keys_values)


def mixer(x, halo, taps, rates, weights, residual):
    width = residual.shape[1]
    steps = width // GROUP
    states = jax.ShapeDtypeStruct((MODES, width // LANES, LANES), jnp.float32)
    by_rows = pl.BlockSpec((ROWS, GROUP), lambda i: (0, i))
    by_modes = pl.BlockSpec((MODES, GROUP), lambda i: (0, i))
    by_state = pl.BlockSpec((MODES, SUB, LANES), lambda i: (0, i, 0))
    return pl.pallas_call(
        mixer_kernel,
        grid=(steps,),
        in_specs=[
            pl.BlockSpec((3, ROWS, GROUP), lambda i: (0, 0, i)),
            pl.BlockSpec((3, SUB, GROUP), lambda i: (0, 0, i)),
            pl.BlockSpec((3, SHORT, GROUP), lambda i: (0, 0, i)),
            by_modes,
            by_modes,
            by_rows,
        ],
        out_specs=[by_rows, pl.BlockSpec((ROWS * SUB, LANES), lambda i: (i, 0)), by_state, by_state, by_state],
        out_shape=[
            jax.ShapeDtypeStruct((ROWS, width), jnp.float32),
            jax.ShapeDtypeStruct((ROWS * width // LANES, LANES), jnp.float32),
            states,
            states,
            states,
        ],
        scratch_shapes=[
            pltpu.VMEM((3, (SUB + ROWS) * SUB, LANES), jnp.float32),
            pltpu.VMEM((3, SUB * SUB, LANES), jnp.float32),
            pltpu.VMEM((2, MODES * SUB, LANES), jnp.float32),
            pltpu.VMEM((ROWS * SUB, LANES), jnp.float32),
            pltpu.VMEM((ROWS * SUB, LANES), jnp.float32),
        ],
        compiler_params=PARAMS,
        cost_estimate=pl.CostEstimate(flops=80_000_000, bytes_accessed=30_000_000, transcendentals=0),
        name="mixer",
    )(x, halo, taps, rates, weights, residual)


def carried(state, rate, weight, base, first, after):
    width = base.shape[1]
    modes = pl.BlockSpec((MODES, SUB, LANES), lambda i: (0, i, 0))
    rows = pl.BlockSpec((ROWS, GROUP), lambda i: (0, i))
    return pl.pallas_call(
        carried_kernel,
        grid=(width // GROUP,),
        in_specs=[modes, modes, modes, rows, pl.BlockSpec((ROWS * SUB, LANES), lambda i: (i, 0)), ANY],
        out_specs=rows,
        out_shape=jax.ShapeDtypeStruct((ROWS, width), jnp.float32),
        scratch_shapes=[
            pltpu.VMEM((MODES, SUB, LANES), jnp.float32),
            pltpu.VMEM((ROWS * SUB, LANES), jnp.float32),
        ],
        compiler_params=PARAMS,
        cost_estimate=pl.CostEstimate(flops=20_000_000, bytes_accessed=12_000_000, transcendentals=0),
        name="carried",
    )(state, rate, weight, base, first, after)


def level(span, which, place, rate, own, others, after):
    state = jax.ShapeDtypeStruct(rate.shape, jnp.float32)
    return pl.pallas_call(
        lambda *refs: level_kernel(span, which, *refs),
        in_specs=[SMEM] + [VMEM] * 5 + [ANY],
        out_specs=[VMEM, VMEM],
        out_shape=[state, state],
        compiler_params=PARAMS,
        cost_estimate=pl.CostEstimate(flops=1_000_000, bytes_accessed=3_000_000, transcendentals=0),
        name="level",
    )(place, rate, own, *others, after)


def entering(place, rate, before_x, before_z, others, after):
    return pl.pallas_call(
        entering_kernel,
        in_specs=[SMEM] + [VMEM] * 6 + [ANY],
        out_specs=VMEM,
        out_shape=jax.ShapeDtypeStruct(rate.shape, jnp.float32),
        compiler_params=PARAMS,
        cost_estimate=pl.CostEstimate(flops=1_000_000, bytes_accessed=3_000_000, transcendentals=0),
        name="entering",
    )(place, rate, before_x, before_z, *others, after)


def attend_scratch():
    return [
        pltpu.VMEM((SUB * ROWS, HEAD), jnp.bfloat16),
        pltpu.VMEM((CHUNK, HEAD), jnp.bfloat16),
        pltpu.VMEM((CHUNK, 2 * HEAD), jnp.bfloat16),
        pltpu.VMEM((SUB * ROWS, 2 * HEAD), jnp.float32),
        pltpu.VMEM((SUB * ROWS, LANES), jnp.float32),
    ]


def attend_near(place, lengths, asked, row, after):
    return pl.pallas_call(
        lambda *refs: attend_kernel(tuple(range(SIDE)), True, *refs),
        in_specs=[SMEM, SMEM] + [VMEM] * (SIDE + 1) + [ANY],
        out_specs=[VMEM, VMEM],
        out_shape=[
            jax.ShapeDtypeStruct((SIDE, SUB * ROWS, 2 * HEAD), jnp.float32),
            jax.ShapeDtypeStruct((SIDE, SUB * ROWS, LANES), jnp.float32),
        ],
        scratch_shapes=attend_scratch(),
        compiler_params=PARAMS,
        cost_estimate=pl.CostEstimate(flops=8_000_000_000, bytes_accessed=15_000_000, transcendentals=3_000_000),
        name="attend_near",
    )(place, lengths, *asked, row, after)


def attend_far(backs, place, lengths, asked, pieces, sums, shift, after):
    q = jax.ShapeDtypeStruct(asked[0].shape, jnp.bfloat16)
    return pl.pallas_call(
        lambda *refs: attend_kernel(backs, False, *refs),
        in_specs=[SMEM, SMEM] + [VMEM] * (len(backs) + SIDE + 1) + [ANY, ANY],
        out_specs=[VMEM] * len(backs),
        out_shape=[q] * len(backs),
        scratch_shapes=attend_scratch(),
        compiler_params=PARAMS,
        cost_estimate=pl.CostEstimate(flops=8_000_000_000, bytes_accessed=15_000_000, transcendentals=3_000_000),
        name="attend_far",
    )(place, lengths, *[asked[r] for r in backs], *pieces, sums, shift, *after)


def squared(place, base, parts):
    return pl.pallas_call(
        squares_kernel,
        in_specs=[SMEM] + [VMEM] * (SIDE + 1),
        out_specs=VMEM,
        out_shape=jax.ShapeDtypeStruct((base.shape[0], 1), jnp.float32),
        compiler_params=PARAMS,
        name="squared",
    )(place, base, *parts)


def streamed(place, base, parts, after):
    wide = jax.ShapeDtypeStruct(base.shape, jnp.bfloat16)
    return pl.pallas_call(
        stream_kernel,
        in_specs=[SMEM] + [VMEM] * (SIDE + 1) + [ANY],
        out_specs=[VMEM, VMEM],
        out_shape=[wide, wide],
        compiler_params=PARAMS,
        cost_estimate=pl.CostEstimate(flops=4_000_000, bytes_accessed=9_000_000, transcendentals=0),
        name="streamed",
    )(place, base, *parts, after)


def normalized(stream, gain, own, other):
    rows, width = stream.shape
    block = pl.BlockSpec((rows, width // SIDE), lambda i: (0, i))
    whole = pl.BlockSpec(own.shape, lambda i: (0, 0))
    return pl.pallas_call(
        lambda *refs: normed_kernel(width, *refs),
        grid=(SIDE,),
        in_specs=[block, pl.BlockSpec((1, width // SIDE), lambda i: (0, i)), whole, whole],
        out_specs=block,
        out_shape=jax.ShapeDtypeStruct(stream.shape, jnp.bfloat16),
        compiler_params=PARAMS,
        name="normalized",
    )(stream, gain, own, other)


def local(streams, short_taps, rates, residues, residual, gain, queries, keys_values, lengths):
    width = residual.shape[1]
    head_cols = width // SIDE
    y, z, x = (lax.axis_index(a) for a in ("y", "z", "x"))
    place = jnp.stack([y, z, x, lax.axis_index("tp")])

    by_stream = streams.transpose(1, 0, 2)
    route = [(i, i + 1) for i in range(SIDE**3 - 1)]
    halo = lax.ppermute(by_stream[:, ROWS - SUB:], ("y", "z", "x"), route)
    near = [turn(value, "y", r) for r, value in enumerate(apart(place, keys_values))]
    asked = [
        turn(lax.dynamic_slice_in_dim(queries, ((y + r) & (SIDE - 1)) * head_cols, head_cols, 1), "y", r)
        for r in range(SIDE)
    ]
    part, halo = lax.optimization_barrier((jnp.stack(near), halo))
    weights = residues * jnp.sqrt(-jnp.expm1(-2.0 * rates))
    row = jnp.stack([turn_cores(part, k, "xz") for k in range(SIDE)])
    halo, after = lax.optimization_barrier((halo, row))
    pieces = [turn_cores(row, m, "zx") for m in range(1, SIDE)]
    base, first, end, rate, weight = mixer(
        by_stream, halo, short_taps.transpose(1, 0, 2), rates, weights, residual
    )
    end, *asked = lax.optimization_barrier((end, *asked))

    def others(value, axis):
        sent = value.astype(jnp.bfloat16)
        return [turn(sent, axis, k) for k in range(1, SIDE)]

    def far(r, *after):
        return attend_far((r,), place, lengths, asked, pieces, sums, shift, after)[0]

    heads, parts = {}, {}
    sums, shift = attend_near(place, lengths, asked, row, end)
    end, sums, shift = lax.optimization_barrier((end, sums, shift))
    others_x = others(end, "x")
    heads[1] = far(1, end, end)
    before_x, total = level(ROWS, 2, place, rate, end, others_x, heads[1])
    others_z = others(total, "z")
    heads[3] = far(3, total, total)
    before_z, total = level(ROWS * SIDE, 1, place, rate, total, others_z, heads[3])
    others_y = others(total, "y")
    heads[2] = far(2, total, total)
    for r in (1, 3):
        parts[r] = turn(heads[r], "y", SIDE - r)
    state = entering(place, rate, before_x, before_z, others_y, heads[2])
    parts[0] = far(0, state, state)
    parts[2] = turn(heads[2], "y", SIDE - 2)
    base = carried(state, rate, weight, base, first, parts[0])
    parts = [parts[r] for r in range(SIDE)]
    own = squared(place, base, parts)
    other = lax.ppermute(own, "tp", [(0, 1), (1, 0)])
    stream, attended = streamed(place, base, parts, own)
    normed = normalized(stream, gain[None], own, other)
    return (stream, normed, attended)


def solution(mesh):
    split = Mesh(mesh.devices.reshape(SIDE, SIDE, SIDE, 2), MESH)
    ctx = MESH[:3]
    in_specs = (
        P(ctx, None, "tp"),
        P(None, None, "tp"),
        P(None, "tp"),
        P(None, "tp"),
        P(ctx, "tp"),
        P("tp"),
        P(ctx, "tp"),
        P(ctx, None, "tp"),
        P(),
    )
    out_specs = (P(ctx, "tp"), P(ctx, "tp"), P(ctx, "tp"))
    return jax.shard_map(local, mesh=split, in_specs=in_specs, out_specs=out_specs, check_vma=False)
```

```python
import math

import jax
import jax.numpy as jnp
from jax import lax
from jax.experimental import pallas as pl
from jax.experimental.pallas import tpu as pltpu
from jax.sharding import Mesh
from jax.sharding import PartitionSpec as P

HEAD = 128
SHORT = 7
MODES = 16
ROWS = 128
SIDE = 4
LANES = 128
SUB = 8
GROUP = SUB * LANES
CHUNK = SIDE * ROWS
SCALE = math.log2(math.e) / math.sqrt(HEAD)
NEG = -1e30
SAFE = 100.0
MESH = ("y", "z", "x", "tp")
VMEM = pl.BlockSpec(memory_space=pltpu.VMEM)
SMEM = pl.BlockSpec(memory_space=pltpu.SMEM)
ANY = pl.BlockSpec(memory_space=pl.ANY)
PARAMS = pltpu.CompilerParams(vmem_limit_bytes=40 * 1024 * 1024)


def spread(moves):
    route = []
    for i in range(2 * SIDE**3):
        y, z, x, core = i // 32, i // 8 % SIDE, i // 2 % SIDE, i % 2
        dy, dz, dx = moves(core)
        y, z, x = (y + dy) % SIDE, (z + dz) % SIDE, (x + dx) % SIDE
        route.append((i, y * 32 + z * 8 + x * 2 + core))
    return route


def turn(value, axis, distance):
    if distance % SIDE == 0:
        return value
    return lax.ppermute(value, axis, [(i, (i + distance) % SIDE) for i in range(SIDE)])


def turn_cores(value, distance, axes):
    if distance == 0:
        return value
    return lax.ppermute(value, MESH, spread(lambda core: tuple(distance * (a == axes[core]) for a in "yzx")))


def apart_kernel(place_ref, kv_ref, *out_refs):
    for r, out_ref in enumerate(out_refs):
        head = (place_ref[0] + r) & (SIDE - 1)
        cols = pl.ds(pl.multiple_of(head * HEAD, HEAD), HEAD)
        for j in range(2):
            out_ref[j] = kv_ref[:, j, cols]


def states_kernel(x_ref, halo_ref, taps_ref, rates_ref, weights_ref,
                  first_ref, gated_ref, end_ref, rate_ref, weight_ref,
                  window, taps, modes):
    for c in range(SUB):
        cols = slice(c * LANES, (c + 1) * LANES)
        for j in range(3):
            window[j, pl.ds(c, SUB, stride=SUB), :] = halo_ref[j, :, cols].astype(jnp.float32)
            window[j, pl.ds(SUB * SUB + c, ROWS, stride=SUB), :] = x_ref[j, :, cols].astype(jnp.float32)
            taps[j, pl.ds(c, SHORT, stride=SUB), :] = taps_ref[j, :, cols]
        modes[0, pl.ds(c, MODES, stride=SUB), :] = rates_ref[:, cols]
        modes[1, pl.ds(c, MODES, stride=SUB), :] = weights_ref[:, cols]
    for n in range(MODES):
        rate_ref[n] = modes[0, n * SUB:(n + 1) * SUB]
        weight_ref[n] = modes[1, n * SUB:(n + 1) * SUB]
    modes[0] = jnp.exp(-modes[0])

    def several(i, states):
        start = i * (SUB * SUB)
        found = []
        for j in range(3):
            tap = [taps[j, k * SUB:(k + 1) * SUB] for k in range(SHORT)]
            seen = [
                window[j, pl.ds(pl.multiple_of(start + (SUB - SHORT + 1 + k) * SUB, SUB), SUB), :]
                for k in range(SUB + SHORT - 1)
            ]
            sums = []
            for u in range(SUB):
                total = tap[0] * seen[SHORT - 1 + u]
                for k in range(1, SHORT):
                    total = total + tap[k] * seen[SHORT - 1 + u - k]
                sums.append(total)
            found.append(sums)
        gated = [found[1][u] * found[2][u] for u in range(SUB)]
        for u in range(SUB):
            rows = pl.ds(pl.multiple_of(start + u * SUB, SUB), SUB)
            first_ref[rows, :] = found[0][u]
            gated_ref[rows, :] = gated[u]
        fresh = []
        for n in range(MODES):
            decay = modes[0, n * SUB:(n + 1) * SUB]
            state = states[n]
            for u in range(SUB):
                state = decay * state + gated[u]
            fresh.append(state)
        return tuple(fresh)

    zero = jnp.zeros((SUB, LANES), jnp.float32)
    states = lax.fori_loop(0, ROWS // SUB, several, (zero,) * MODES)
    for n in range(MODES):
        end_ref[n] = states[n]


def mixed_kernel(state_ref, rate_ref, weight_ref, gated_ref, first_ref, residual_ref, after_ref, last_ref,
                 base_ref, decay, out):
    decay[...] = jnp.exp(-rate_ref[...])

    def step(t, states):
        rows = pl.ds(pl.multiple_of(t * SUB, SUB), SUB)
        g = gated_ref[rows, :]
        fresh, sums = [], [None, None]
        for n in range(MODES):
            state = decay[n] * states[n] + g
            fresh.append(state)
            part = weight_ref[n] * state
            sums[n % 2] = part if sums[n % 2] is None else sums[n % 2] + part
        out[rows, :] = (sums[0] + sums[1]) * first_ref[rows, :]
        return tuple(fresh)

    lax.fori_loop(0, ROWS, step, tuple(state_ref[n] for n in range(MODES)), unroll=4)
    for c in range(SUB):
        cols = slice(c * LANES, (c + 1) * LANES)
        base_ref[:, cols] = residual_ref[:, cols].astype(jnp.float32) + out[pl.ds(c, ROWS, stride=SUB), :]


def level_kernel(span, which, place_ref, rate_ref, own_ref, one_ref, two_ref, three_ref, after_ref, before_ref, total_ref):
    place = place_ref[which]

    def one(n, unused):
        rate = rate_ref[n] * float(span)
        total = own_ref[n] * jnp.exp(-rate * (SIDE - 1 - place).astype(jnp.float32))
        before = jnp.zeros_like(total)
        for k, ref in enumerate((one_ref, two_ref, three_ref), 1):
            other = ref[n].astype(jnp.float32)
            origin = (place - k) & (SIDE - 1)
            total = total + other * jnp.exp(-rate * (SIDE - 1 - origin).astype(jnp.float32))
            kept = other if k == 1 else other * jnp.exp(-rate * float(k - 1))
            before = before + kept * jnp.where(place >= k, 1.0, 0.0)
        before_ref[n] = before
        total_ref[n] = total
        return unused

    lax.fori_loop(0, MODES, one, 0)


def entering_kernel(place_ref, rate_ref, x_ref, z_ref, one_ref, two_ref, three_ref, after_ref, state_ref):
    y, z, x = place_ref[0], place_ref[1], place_ref[2]

    def one(n, unused):
        rate = rate_ref[n] * float(ROWS)
        before = jnp.zeros_like(rate)
        for k, ref in enumerate((one_ref, two_ref, three_ref), 1):
            kept = ref[n].astype(jnp.float32) * jnp.exp(-rate * float(SIDE * SIDE * (k - 1)))
            before = before + kept * jnp.where(y >= k, 1.0, 0.0)
        state_ref[n] = (
            x_ref[n]
            + jnp.exp(-rate * x.astype(jnp.float32)) * z_ref[n]
            + jnp.exp(-rate * (SIDE * z + x).astype(jnp.float32)) * before
        )
        return unused

    lax.fori_loop(0, MODES, one, 0)


def attend_kernel(backs, near, at, place_ref, lengths_ref, *refs):
    count = len(backs)
    refs = list(refs)
    q_refs = [refs.pop(0) for _ in backs]
    pieces = [refs.pop(0) for _ in range(1 if near else SIDE)]
    if near:
        refs.pop(0)
        refs.pop(0)
        sums_ref, shift_ref = refs.pop(0), refs.pop(0)
    else:
        sums_in, shift_in = refs.pop(0), refs.pop(0)
        refs.pop(0)
        refs.pop(0)
        o_refs = [refs.pop(0) for _ in backs]
    q_rows, keys, values, accum, largest, highest = refs
    y, z, x, core = place_ref[0], place_ref[1], place_ref[2], place_ref[3]
    bounds = []
    total = 0
    for i in range(4):
        total = total + lengths_ref[i]
        bounds.append(total)

    def document_start(position):
        start = jnp.zeros_like(position)
        for bound in bounds:
            start = jnp.maximum(start, jnp.where(position >= bound, bound, 0))
        return start

    values[:, HEAD:] = jnp.ones((CHUNK, HEAD), jnp.bfloat16)

    def query(s, unused):
        back = jnp.int32(backs[0])
        for i in range(1, count):
            back = jnp.where(s == i, backs[i], back)
        query_block = 16 * ((y - back) & (SIDE - 1)) + SIDE * z + x
        query_first = query_block * ROWS
        last_start = document_start(query_first + ROWS - 1)
        low = document_start(query_first) // ROWS

        plane, row = query_block >> 4, query_block >> 2

        def near_below(block):
            by_row = 4 * (block >> 4) + jnp.clip((block & 15) - 4 * z, 0, SIDE)
            return jnp.where(core == 0, by_row, (block + 3 - x) >> 2)

        found = near_below(query_block + 1) - near_below(low)
        if not near:
            found = query_block - low + 1 - found

        def block_of(i):
            if near:
                here = jnp.where(core == 0, x, z)
                j = i - here - 1
                below, left = 16 * (plane - 1 - (j >> 2)), 3 - (j & 3)
                mine = query_block - jnp.where(core == 0, i, 4 * i)
                other = below + jnp.where(core == 0, 4 * z + left, 4 * left + x)
                block = jnp.where(i <= here, mine, other)
            else:
                j = (i >> 2) - z
                left = 3 - lax.rem(j, 3)
                left = left - jnp.where(left <= z, 1, 0)
                above = 4 * (4 * (plane - 1 - j // 3) + left)
                by_row = jnp.where(j < 0, 16 * plane + 4 * (z - 1 - (i >> 2)), above) + 3 - (i & 3)
                k = i - x
                left = 3 - lax.rem(k, 3)
                left = left - jnp.where(left <= x, 1, 0)
                by_column = jnp.where(k < 0, query_block - 1 - i, 4 * (row - 1 - k // 3) + left)
                block = jnp.where(core == 0, by_row, by_column)
            return jnp.where(i < found, block, -1)

        chunks = (found + SIDE - 1) // SIDE

        def fetch(chunk):
            for i in range(SIDE):
                block = jnp.maximum(block_of(chunk * SIDE + i), 0)
                turned = (y - (block >> 4)) & (SIDE - 1)
                behind_z = (z - (block >> 2)) & (SIDE - 1)
                behind_x = (x - block) & (SIDE - 1)
                outer = jnp.where(core == 0, behind_z, behind_x)
                inner = jnp.where(core == 0, behind_x, behind_z)
                rows = slice(i * ROWS, (i + 1) * ROWS)

                def pair(source, k):
                    keys[rows] = source[k, turned, 0]
                    values[rows, :HEAD] = source[k, turned, 1]

                if near:
                    pair(pieces[0], inner)
                else:
                    half = SIDE // 2
                    pl.when(outer <= 1)(lambda: pair(pieces[0], inner))
                    pl.when((outer == 2) & (inner < half))(lambda: pair(pieces[1], inner))
                    pl.when((outer == 2) & (inner >= half))(lambda: pair(pieces[2], inner - half))
                    pl.when(outer == 3)(lambda: pair(pieces[3], inner))

        for i in range(count):
            @pl.when(s == i)
            def _():
                for g in range(SUB):
                    q_rows[g * ROWS:(g + 1) * ROWS] = q_refs[i][:, g * HEAD:(g + 1) * HEAD]

        def scored():
            return lax.dot_general(
                q_rows[...], keys[...], (((1,), (1,)), ((), ())), preferred_element_type=jnp.float32
            )

        def masked(scores, chunk):
            query_pos = query_first + lax.broadcasted_iota(jnp.int32, (ROWS, ROWS), 0)
            start = document_start(query_pos)
            lane = lax.broadcasted_iota(jnp.int32, (ROWS, ROWS), 1)
            parts = []
            for i in range(SIDE):
                key_pos = block_of(chunk * SIDE + i) * ROWS + lane
                parts.append(jnp.where((key_pos <= query_pos) & (key_pos >= start), 0.0, NEG))
            bias = jnp.concatenate(parts, axis=1)
            return (scores.reshape(SUB, ROWS, CHUNK) + bias[None]).reshape(SUB * ROWS, CHUNK)

        def begin():
            if near:
                accum[...] = jnp.zeros_like(accum)
                own = pieces[0][0, back, 0].astype(jnp.float32) * SCALE
                paired = q_rows[...].astype(jnp.float32).reshape(SUB, ROWS, HEAD) * own[None]
                largest[...] = jnp.dot(
                    paired.reshape(SUB * ROWS, HEAD).astype(jnp.bfloat16),
                    jnp.ones((HEAD, LANES), jnp.bfloat16),
                    preferred_element_type=jnp.float32,
                )
            else:
                accum[...] = sums_in[at]
                largest[...] = shift_in[at]

        def weighed(scores, shift):
            parts = [scores[:, i * LANES:(i + 1) * LANES] * SCALE - shift for i in range(SIDE)]
            weights = jnp.concatenate([jnp.exp2(p).astype(jnp.bfloat16) for p in parts], axis=1)
            high = jnp.maximum(jnp.maximum(parts[0], parts[1]), jnp.maximum(parts[2], parts[3]))
            return jnp.dot(weights, values[...], preferred_element_type=jnp.float32), high

        def quick(chunk, carry):
            fetch(chunk)

            def update(scores):
                added, high = weighed(scores, largest[...])
                accum[...] += added
                highest[...] = jnp.maximum(highest[...], jnp.max(high.reshape(ROWS, SUB, LANES), axis=0))

            whole = (block_of(chunk * SIDE) < query_block) & (block_of(chunk * SIDE + SIDE - 1) * ROWS >= last_start)
            pl.when(whole)(lambda: update(scored()))
            pl.when(jnp.logical_not(whole))(lambda: update(masked(scored(), chunk)))
            return carry

        def careful(chunk, carry):
            fetch(chunk)
            scores = masked(scored(), chunk)
            before = largest[...]
            fresh = jnp.maximum(before, SCALE * jnp.max(scores, axis=1, keepdims=True))
            shrink = jnp.exp2(before - fresh)
            largest[...] = fresh
            added = weighed(scores, fresh)[0]
            accum[...] = accum[...] * jnp.concatenate([shrink, shrink], axis=1) + added
            return carry

        begin()
        highest[...] = jnp.full_like(highest, NEG)
        lax.fori_loop(0, chunks, quick, 0)

        @pl.when(jnp.logical_not(jnp.max(highest[...]) < SAFE))
        def _():
            begin()
            lax.fori_loop(0, chunks, careful, 0)

        if near:
            sums_ref[s] = accum[...]
            shift_ref[s] = largest[...]
        else:
            for i in range(count):
                @pl.when(s == i)
                def _():
                    for g in range(SUB):
                        rows = slice(g * ROWS, (g + 1) * ROWS)
                        o_refs[i][:, g * HEAD:(g + 1) * HEAD] = (
                            accum[rows, :HEAD] / accum[rows, HEAD:]
                        ).astype(jnp.bfloat16)
        return unused

    lax.fori_loop(0, count, query, 0)


def joined(place_ref, base_ref, parts, store):
    rows, width = base_ref.shape
    cols = width // SIDE
    for r, part in enumerate(parts):
        start = pl.multiple_of(((place_ref[0] + r) & (SIDE - 1)) * cols, cols)
        heads = part[...]
        stream = base_ref[:, pl.ds(start, cols)] + heads.astype(jnp.float32)
        store(pl.ds(start, cols), heads, stream.astype(jnp.bfloat16))


def squares_kernel(place_ref, base_ref, p0, p1, p2, p3, squares_ref):
    squares_ref[...] = jnp.zeros_like(squares_ref)

    def store(cols, heads, stream):
        wide = stream.astype(jnp.float32)
        squares_ref[...] += jnp.sum(wide * wide, axis=1, keepdims=True)

    joined(place_ref, base_ref, (p0, p1, p2, p3), store)


def stream_kernel(place_ref, base_ref, p0, p1, p2, p3, squares_ref, stream_ref, attended_ref):
    def store(cols, heads, stream):
        attended_ref[:, cols] = heads
        stream_ref[:, cols] = stream

    joined(place_ref, base_ref, (p0, p1, p2, p3), store)


def normed_kernel(width, stream_ref, gain_ref, own_ref, other_ref, normed_ref):
    factor = lax.rsqrt((own_ref[...] + other_ref[...]) / (2 * width) + 1e-06)
    normed_ref[...] = (stream_ref[...].astype(jnp.float32) * factor * gain_ref[...]).astype(jnp.bfloat16)


def apart(place, keys_values):
    return pl.pallas_call(
        apart_kernel,
        in_specs=[SMEM, VMEM],
        out_specs=[VMEM] * SIDE,
        out_shape=[jax.ShapeDtypeStruct((2, ROWS, HEAD), jnp.bfloat16)] * SIDE,
        compiler_params=PARAMS,
        name="apart",
    )(place, keys_values)


def mode_states(x, halo, taps, rates, weights, before):
    width = rates.shape[1]
    steps = width // GROUP // 2
    skip = steps if before else 0
    by_modes = pl.BlockSpec((MODES, GROUP), lambda i: (0, i + skip))
    by_state = pl.BlockSpec((MODES, SUB, LANES), lambda i: (0, i + skip, 0))
    by_time = pl.BlockSpec((ROWS * SUB, LANES), lambda i: (i + skip, 0))
    turned = jax.ShapeDtypeStruct((ROWS * width // LANES, LANES), jnp.float32)
    states = jax.ShapeDtypeStruct((MODES, width // LANES, LANES), jnp.float32)
    count = len(before)

    def kernel(*refs):
        states_kernel(*refs[:5], *refs[5 + count:])

    return pl.pallas_call(
        kernel,
        grid=(steps,),
        in_specs=[
            pl.BlockSpec((3, ROWS, GROUP), lambda i: (0, 0, i + skip)),
            pl.BlockSpec((3, SUB, GROUP), lambda i: (0, 0, i + skip)),
            pl.BlockSpec((3, SHORT, GROUP), lambda i: (0, 0, i + skip)),
            by_modes,
            by_modes,
        ] + [ANY] * count,
        input_output_aliases={5 + i: i for i in range(count)},
        out_specs=[by_time, by_time, by_state, by_state, by_state],
        out_shape=[turned, turned, states, states, states],
        scratch_shapes=[
            pltpu.VMEM((3, (SUB + ROWS) * SUB, LANES), jnp.float32),
            pltpu.VMEM((3, SUB * SUB, LANES), jnp.float32),
            pltpu.VMEM((2, MODES * SUB, LANES), jnp.float32),
        ],
        compiler_params=PARAMS,
        cost_estimate=pl.CostEstimate(flops=30_000_000, bytes_accessed=10_000_000, transcendentals=0),
        name="mode_states",
    )(x, halo, taps, rates, weights, *before)


def mixed(state, rate, weight, gated, first, residual, after):
    rows, width = residual.shape
    modes = pl.BlockSpec((MODES, SUB, LANES), lambda i: (0, i, 0))
    by_time = pl.BlockSpec((ROWS * SUB, LANES), lambda i: (i, 0))
    by_rows = pl.BlockSpec((ROWS, GROUP), lambda i: (0, i))
    return pl.pallas_call(
        mixed_kernel,
        grid=(width // GROUP,),
        in_specs=[modes, modes, modes, by_time, by_time, by_rows, ANY, ANY],
        out_specs=by_rows,
        out_shape=jax.ShapeDtypeStruct((rows, width), jnp.float32),
        scratch_shapes=[
            pltpu.VMEM((MODES, SUB, LANES), jnp.float32),
            pltpu.VMEM((ROWS * SUB, LANES), jnp.float32),
        ],
        compiler_params=PARAMS,
        cost_estimate=pl.CostEstimate(flops=40_000_000, bytes_accessed=20_000_000, transcendentals=0),
        name="mixed",
    )(state, rate, weight, gated, first, residual, *after)


def level(span, which, place, rate, own, others, after):
    state = jax.ShapeDtypeStruct(rate.shape, jnp.float32)
    return pl.pallas_call(
        lambda *refs: level_kernel(span, which, *refs),
        in_specs=[SMEM] + [VMEM] * 5 + [ANY],
        out_specs=[VMEM, VMEM],
        out_shape=[state, state],
        compiler_params=PARAMS,
        cost_estimate=pl.CostEstimate(flops=1_000_000, bytes_accessed=3_000_000, transcendentals=0),
        name="level",
    )(place, rate, own, *others, after)


def entering(place, rate, before_x, before_z, others, after):
    return pl.pallas_call(
        entering_kernel,
        in_specs=[SMEM] + [VMEM] * 6 + [ANY],
        out_specs=VMEM,
        out_shape=jax.ShapeDtypeStruct(rate.shape, jnp.float32),
        compiler_params=PARAMS,
        cost_estimate=pl.CostEstimate(flops=1_000_000, bytes_accessed=3_000_000, transcendentals=0),
        name="entering",
    )(place, rate, before_x, before_z, *others, after)


def attend_scratch():
    return [
        pltpu.VMEM((SUB * ROWS, HEAD), jnp.bfloat16),
        pltpu.VMEM((CHUNK, HEAD), jnp.bfloat16),
        pltpu.VMEM((CHUNK, 2 * HEAD), jnp.bfloat16),
        pltpu.VMEM((SUB * ROWS, 2 * HEAD), jnp.float32),
        pltpu.VMEM((SUB * ROWS, LANES), jnp.float32),
        pltpu.VMEM((SUB, LANES), jnp.float32),
    ]


def attend_near(backs, place, lengths, asked, row, after):
    count = len(backs)
    return pl.pallas_call(
        lambda *refs: attend_kernel(backs, True, None, *refs),
        in_specs=[SMEM, SMEM] + [VMEM] * (count + 1) + [ANY, ANY],
        out_specs=[VMEM, VMEM],
        out_shape=[
            jax.ShapeDtypeStruct((count, SUB * ROWS, 2 * HEAD), jnp.float32),
            jax.ShapeDtypeStruct((count, SUB * ROWS, LANES), jnp.float32),
        ],
        scratch_shapes=attend_scratch(),
        compiler_params=PARAMS,
        cost_estimate=pl.CostEstimate(flops=4_000_000_000, bytes_accessed=10_000_000, transcendentals=3_000_000),
        name="attend_near",
    )(place, lengths, *[asked[r] for r in backs], row, *after)


def attend_far(back, at, place, lengths, q, pieces, sums, shift, after):
    return pl.pallas_call(
        lambda *refs: attend_kernel((back,), False, at, *refs),
        in_specs=[SMEM, SMEM] + [VMEM] * (SIDE + 3) + [ANY, ANY],
        out_specs=VMEM,
        out_shape=jax.ShapeDtypeStruct(q.shape, jnp.bfloat16),
        scratch_shapes=attend_scratch(),
        compiler_params=PARAMS,
        cost_estimate=pl.CostEstimate(flops=4_000_000_000, bytes_accessed=10_000_000, transcendentals=3_000_000),
        name="attend_far",
    )(place, lengths, q, *pieces, sums, shift, *after)


def squared(place, base, parts):
    return pl.pallas_call(
        squares_kernel,
        in_specs=[SMEM] + [VMEM] * (SIDE + 1),
        out_specs=VMEM,
        out_shape=jax.ShapeDtypeStruct((base.shape[0], 1), jnp.float32),
        compiler_params=PARAMS,
        name="squared",
    )(place, base, *parts)


def streamed(place, base, parts, after):
    wide = jax.ShapeDtypeStruct(base.shape, jnp.bfloat16)
    return pl.pallas_call(
        stream_kernel,
        in_specs=[SMEM] + [VMEM] * (SIDE + 1) + [ANY],
        out_specs=[VMEM, VMEM],
        out_shape=[wide, wide],
        compiler_params=PARAMS,
        cost_estimate=pl.CostEstimate(flops=4_000_000, bytes_accessed=9_000_000, transcendentals=0),
        name="streamed",
    )(place, base, *parts, after)


def normalized(stream, gain, own, other):
    rows, width = stream.shape
    block = pl.BlockSpec((rows, width // SIDE), lambda i: (0, i))
    whole = pl.BlockSpec(own.shape, lambda i: (0, 0))
    return pl.pallas_call(
        lambda *refs: normed_kernel(width, *refs),
        grid=(SIDE,),
        in_specs=[block, pl.BlockSpec((1, width // SIDE), lambda i: (0, i)), whole, whole],
        out_specs=block,
        out_shape=jax.ShapeDtypeStruct(stream.shape, jnp.bfloat16),
        compiler_params=PARAMS,
        name="normalized",
    )(stream, gain, own, other)


def local(streams, short_taps, rates, residues, residual, gain, queries, keys_values, lengths):
    width = residual.shape[1]
    head_cols = width // SIDE
    y, z, x = (lax.axis_index(a) for a in ("y", "z", "x"))
    place = jnp.stack([y, z, x, lax.axis_index("tp")])

    by_stream = streams.transpose(1, 0, 2)
    route = [(i, i + 1) for i in range(SIDE**3 - 1)]
    halo = lax.ppermute(by_stream[:, ROWS - SUB:], ("y", "z", "x"), route)
    near = [turn(value, "y", r) for r, value in enumerate(apart(place, keys_values))]
    asked = [
        turn(lax.dynamic_slice_in_dim(queries, ((y + r) & (SIDE - 1)) * head_cols, head_cols, 1), "y", r)
        for r in range(SIDE)
    ]
    part, halo = lax.optimization_barrier((jnp.stack(near), halo))
    weights = residues * jnp.sqrt(-jnp.expm1(-2.0 * rates))
    row = jnp.stack([turn_cores(part, k, "xz") for k in range(SIDE)])
    taps = short_taps.transpose(1, 0, 2)
    partial = mode_states(by_stream, halo, taps, rates, weights, ())
    row, asked[1], asked[3], end = lax.optimization_barrier((row, asked[1], asked[3], partial[2]))
    halo, _ = lax.optimization_barrier((halo, row))
    left, right = turn_cores(row, 1, "zx"), turn_cores(row, SIDE - 1, "zx")
    first, gated, end, rate, weight = mode_states(
        by_stream, halo, taps, rates, weights, (*partial[:2], end, *partial[3:])
    )

    def others(value, axis):
        sent = value.astype(jnp.bfloat16)
        return [turn(sent, axis, k) for k in range(1, SIDE)]

    def far(r, at, sums, *after):
        return attend_far(r, at, place, lengths, asked[r], pieces, *sums, after)

    end, asked[2] = lax.optimization_barrier((end, asked[2]))
    others_x = others(end, "x")
    half = SIDE // 2
    pieces = [left, turn_cores(left[:half], 1, "zx"), turn_cores(right[half:], SIDE - 1, "zx"), right]
    odd = attend_near((1, 3), place, lengths, asked, row, (left, right))
    before_x, total = level(ROWS, 2, place, rate, end, others_x, odd[1])
    others_z = others(total, "z")
    even = attend_near((2, 0), place, lengths, asked, row, (total, odd[1]))
    before_z, total = level(ROWS * SIDE, 1, place, rate, total, others_z, even[1])
    others_y = others(total, "y")
    parts = [None] * SIDE
    parts[1] = far(1, 0, odd, total, total)
    state = entering(place, rate, before_x, before_z, others_y, parts[1])
    parts[3] = far(3, 1, odd, state, parts[1])
    parts[1], parts[3] = lax.optimization_barrier((parts[1], parts[3]))
    parts[2] = far(2, 0, even, parts[3], parts[3])
    parts[0] = far(0, 1, even, parts[2], parts[2])
    for r in (1, 3):
        parts[r] = turn(parts[r], "y", SIDE - r)
    base = mixed(state, rate, weight, gated, first, residual, (parts[1], parts[3]))
    parts[0], parts[2] = lax.optimization_barrier((parts[0], parts[2]))
    parts[2] = turn(parts[2], "y", SIDE - 2)
    own = squared(place, base, parts)
    other = lax.ppermute(own, "tp", [(0, 1), (1, 0)])
    stream, attended = streamed(place, base, parts, own)
    normed = normalized(stream, gain[None], own, other)
    return (stream, normed, attended)


def solution(mesh):
    split = Mesh(mesh.devices.reshape(SIDE, SIDE, SIDE, 2), MESH)
    ctx = MESH[:3]
    in_specs = (
        P(ctx, None, "tp"),
        P(None, None, "tp"),
        P(None, "tp"),
        P(None, "tp"),
        P(ctx, "tp"),
        P("tp"),
        P(ctx, "tp"),
        P(ctx, None, "tp"),
        P(),
    )
    out_specs = (P(ctx, "tp"), P(ctx, "tp"), P(ctx, "tp"))
    return jax.shard_map(local, mesh=split, in_specs=in_specs, out_specs=out_specs, check_vma=False)
```

```python
import math

import jax
import jax.numpy as jnp
from jax import lax
from jax.experimental import pallas as pl
from jax.experimental.pallas import tpu as pltpu
from jax.sharding import Mesh
from jax.sharding import PartitionSpec as P

HEAD = 128
SHORT = 7
MODES = 16
ROWS = 128
SIDE = 4
LANES = 128
SUB = 8
GROUP = SUB * LANES
CHUNK = SIDE * ROWS
SCALE = math.log2(math.e) / math.sqrt(HEAD)
NEG = -1e30
SAFE = 100.0
MESH = ("y", "z", "x", "tp")
VMEM = pl.BlockSpec(memory_space=pltpu.VMEM)
SMEM = pl.BlockSpec(memory_space=pltpu.SMEM)
ANY = pl.BlockSpec(memory_space=pl.ANY)
PARAMS = pltpu.CompilerParams(vmem_limit_bytes=40 * 1024 * 1024)


def spread(moves):
    route = []
    for i in range(2 * SIDE**3):
        y, z, x, core = i // 32, i // 8 % SIDE, i // 2 % SIDE, i % 2
        dy, dz, dx = moves(core)
        y, z, x = (y + dy) % SIDE, (z + dz) % SIDE, (x + dx) % SIDE
        route.append((i, y * 32 + z * 8 + x * 2 + core))
    return route


def turn(value, axis, distance):
    if distance % SIDE == 0:
        return value
    return lax.ppermute(value, axis, [(i, (i + distance) % SIDE) for i in range(SIDE)])


def turn_cores(value, distance, axes):
    if distance == 0:
        return value
    return lax.ppermute(value, MESH, spread(lambda core: tuple(distance * (a == axes[core]) for a in "yzx")))


def apart_kernel(place_ref, kv_ref, *out_refs):
    for r, out_ref in enumerate(out_refs):
        head = (place_ref[0] + r) & (SIDE - 1)
        cols = pl.ds(pl.multiple_of(head * HEAD, HEAD), HEAD)
        for j in range(2):
            out_ref[j] = kv_ref[:, j, cols]


def states_kernel(x_ref, halo_ref, taps_ref, rates_ref, weights_ref,
                  first_ref, gated_ref, end_ref, rate_ref, weight_ref,
                  window, taps, modes):
    for c in range(SUB):
        cols = slice(c * LANES, (c + 1) * LANES)
        for j in range(3):
            window[j, pl.ds(c, SUB, stride=SUB), :] = halo_ref[j, :, cols].astype(jnp.float32)
            window[j, pl.ds(SUB * SUB + c, ROWS, stride=SUB), :] = x_ref[j, :, cols].astype(jnp.float32)
            taps[j, pl.ds(c, SHORT, stride=SUB), :] = taps_ref[j, :, cols]
        modes[0, pl.ds(c, MODES, stride=SUB), :] = rates_ref[:, cols]
        modes[1, pl.ds(c, MODES, stride=SUB), :] = weights_ref[:, cols]
    for n in range(MODES):
        rate_ref[n] = modes[0, n * SUB:(n + 1) * SUB]
        weight_ref[n] = modes[1, n * SUB:(n + 1) * SUB]
    modes[0] = jnp.exp(-modes[0])

    def several(i, states):
        start = i * (SUB * SUB)
        found = []
        for j in range(3):
            tap = [taps[j, k * SUB:(k + 1) * SUB] for k in range(SHORT)]
            seen = [
                window[j, pl.ds(pl.multiple_of(start + (SUB - SHORT + 1 + k) * SUB, SUB), SUB), :]
                for k in range(SUB + SHORT - 1)
            ]
            sums = []
            for u in range(SUB):
                total = tap[0] * seen[SHORT - 1 + u]
                for k in range(1, SHORT):
                    total = total + tap[k] * seen[SHORT - 1 + u - k]
                sums.append(total)
            found.append(sums)
        gated = [found[1][u] * found[2][u] for u in range(SUB)]
        for u in range(SUB):
            rows = pl.ds(pl.multiple_of(start + u * SUB, SUB), SUB)
            first_ref[rows, :] = found[0][u]
            gated_ref[rows, :] = gated[u]
        fresh = []
        for n in range(MODES):
            decay = modes[0, n * SUB:(n + 1) * SUB]
            state = states[n]
            for u in range(SUB):
                state = decay * state + gated[u]
            fresh.append(state)
        return tuple(fresh)

    zero = jnp.zeros((SUB, LANES), jnp.float32)
    states = lax.fori_loop(0, ROWS // SUB, several, (zero,) * MODES)
    for n in range(MODES):
        end_ref[n] = states[n]


def mixed_kernel(state_ref, rate_ref, weight_ref, gated_ref, first_ref, residual_ref, after_ref, last_ref,
                 base_ref, decay, out):
    decay[...] = jnp.exp(-rate_ref[...])

    def step(t, states):
        rows = pl.ds(pl.multiple_of(t * SUB, SUB), SUB)
        g = gated_ref[rows, :]
        fresh, sums = [], [None, None]
        for n in range(MODES):
            state = decay[n] * states[n] + g
            fresh.append(state)
            part = weight_ref[n] * state
            sums[n % 2] = part if sums[n % 2] is None else sums[n % 2] + part
        out[rows, :] = (sums[0] + sums[1]) * first_ref[rows, :]
        return tuple(fresh)

    lax.fori_loop(0, ROWS, step, tuple(state_ref[n] for n in range(MODES)), unroll=4)
    for c in range(SUB):
        cols = slice(c * LANES, (c + 1) * LANES)
        base_ref[:, cols] = residual_ref[:, cols].astype(jnp.float32) + out[pl.ds(c, ROWS, stride=SUB), :]


def level_kernel(span, which, place_ref, rate_ref, own_ref, one_ref, two_ref, three_ref, after_ref, before_ref, total_ref):
    place = place_ref[which]

    def one(n, unused):
        rate = rate_ref[n] * float(span)
        total = own_ref[n] * jnp.exp(-rate * (SIDE - 1 - place).astype(jnp.float32))
        before = jnp.zeros_like(total)
        for k, ref in enumerate((one_ref, two_ref, three_ref), 1):
            other = ref[n].astype(jnp.float32)
            origin = (place - k) & (SIDE - 1)
            total = total + other * jnp.exp(-rate * (SIDE - 1 - origin).astype(jnp.float32))
            kept = other if k == 1 else other * jnp.exp(-rate * float(k - 1))
            before = before + kept * jnp.where(place >= k, 1.0, 0.0)
        before_ref[n] = before
        total_ref[n] = total
        return unused

    lax.fori_loop(0, MODES, one, 0)


def entering_kernel(place_ref, rate_ref, x_ref, z_ref, one_ref, two_ref, three_ref, after_ref, state_ref):
    y, z, x = place_ref[0], place_ref[1], place_ref[2]

    def one(n, unused):
        rate = rate_ref[n] * float(ROWS)
        before = jnp.zeros_like(rate)
        for k, ref in enumerate((one_ref, two_ref, three_ref), 1):
            kept = ref[n].astype(jnp.float32) * jnp.exp(-rate * float(SIDE * SIDE * (k - 1)))
            before = before + kept * jnp.where(y >= k, 1.0, 0.0)
        state_ref[n] = (
            x_ref[n]
            + jnp.exp(-rate * x.astype(jnp.float32)) * z_ref[n]
            + jnp.exp(-rate * (SIDE * z + x).astype(jnp.float32)) * before
        )
        return unused

    lax.fori_loop(0, MODES, one, 0)


def attend_kernel(backs, near, place_ref, lengths_ref, *refs):
    count = len(backs)
    refs = list(refs)
    q_refs = [refs.pop(0) for _ in backs]
    pieces = [refs.pop(0) for _ in range(1 if near else SIDE)]
    if near:
        refs.pop(0)
        refs.pop(0)
        sums_ref, shift_ref = refs.pop(0), refs.pop(0)
    else:
        sums_in, shift_in = refs.pop(0), refs.pop(0)
        refs.pop(0)
        refs.pop(0)
        o_refs = [refs.pop(0) for _ in backs]
    q_rows, keys, values, accum, largest, highest = refs
    y, z, x, core = place_ref[0], place_ref[1], place_ref[2], place_ref[3]
    bounds = []
    total = 0
    for i in range(4):
        total = total + lengths_ref[i]
        bounds.append(total)

    def document_start(position):
        start = jnp.zeros_like(position)
        for bound in bounds:
            start = jnp.maximum(start, jnp.where(position >= bound, bound, 0))
        return start

    values[:, HEAD:] = jnp.ones((CHUNK, HEAD), jnp.bfloat16)

    def query(s, unused):
        sums, shift = (sums_ref.at[s], shift_ref.at[s]) if near else (accum, largest)
        back = jnp.int32(backs[0])
        for i in range(1, count):
            back = jnp.where(s == i, backs[i], back)
        query_block = 16 * ((y - back) & (SIDE - 1)) + SIDE * z + x
        query_first = query_block * ROWS
        last_start = document_start(query_first + ROWS - 1)
        low = document_start(query_first) // ROWS

        plane, row = query_block >> 4, query_block >> 2

        def near_below(block):
            by_row = 4 * (block >> 4) + jnp.clip((block & 15) - 4 * z, 0, SIDE)
            return jnp.where(core == 0, by_row, (block + 3 - x) >> 2)

        found = near_below(query_block + 1) - near_below(low)
        if not near:
            found = query_block - low + 1 - found

        def block_of(i):
            if near:
                here = jnp.where(core == 0, x, z)
                j = i - here - 1
                below, left = 16 * (plane - 1 - (j >> 2)), 3 - (j & 3)
                mine = query_block - jnp.where(core == 0, i, 4 * i)
                other = below + jnp.where(core == 0, 4 * z + left, 4 * left + x)
                block = jnp.where(i <= here, mine, other)
            else:
                j = (i >> 2) - z
                left = 3 - lax.rem(j, 3)
                left = left - jnp.where(left <= z, 1, 0)
                above = 4 * (4 * (plane - 1 - j // 3) + left)
                by_row = jnp.where(j < 0, 16 * plane + 4 * (z - 1 - (i >> 2)), above) + 3 - (i & 3)
                k = i - x
                left = 3 - lax.rem(k, 3)
                left = left - jnp.where(left <= x, 1, 0)
                by_column = jnp.where(k < 0, query_block - 1 - i, 4 * (row - 1 - k // 3) + left)
                block = jnp.where(core == 0, by_row, by_column)
            return jnp.where(i < found, block, -1)

        chunks = (found + SIDE - 1) // SIDE

        def fetch(chunk):
            for i in range(SIDE):
                block = jnp.maximum(block_of(chunk * SIDE + i), 0)
                turned = (y - (block >> 4)) & (SIDE - 1)
                behind_z = (z - (block >> 2)) & (SIDE - 1)
                behind_x = (x - block) & (SIDE - 1)
                outer = jnp.where(core == 0, behind_z, behind_x)
                inner = jnp.where(core == 0, behind_x, behind_z)
                rows = slice(i * ROWS, (i + 1) * ROWS)

                def pair(source, k):
                    keys[rows] = source[k, turned, 0]
                    values[rows, :HEAD] = source[k, turned, 1]

                if near:
                    pair(pieces[0], inner)
                else:
                    half = SIDE // 2
                    pl.when(outer <= 1)(lambda: pair(pieces[0], inner))
                    pl.when((outer == 2) & (inner < half))(lambda: pair(pieces[1], inner))
                    pl.when((outer == 2) & (inner >= half))(lambda: pair(pieces[2], inner - half))
                    pl.when(outer == 3)(lambda: pair(pieces[3], inner))

        for i in range(count):
            @pl.when(s == i)
            def _():
                for g in range(SUB):
                    q_rows[g * ROWS:(g + 1) * ROWS] = q_refs[i][:, g * HEAD:(g + 1) * HEAD]

        def scored():
            return lax.dot_general(
                q_rows[...], keys[...], (((1,), (1,)), ((), ())), preferred_element_type=jnp.float32
            )

        def masked(scores, chunk):
            query_pos = query_first + lax.broadcasted_iota(jnp.int32, (ROWS, ROWS), 0)
            start = document_start(query_pos)
            lane = lax.broadcasted_iota(jnp.int32, (ROWS, ROWS), 1)
            parts = []
            for i in range(SIDE):
                key_pos = block_of(chunk * SIDE + i) * ROWS + lane
                parts.append(jnp.where((key_pos <= query_pos) & (key_pos >= start), 0.0, NEG))
            bias = jnp.concatenate(parts, axis=1)
            return (scores.reshape(SUB, ROWS, CHUNK) + bias[None]).reshape(SUB * ROWS, CHUNK)

        def begin():
            if near:
                sums[...] = jnp.zeros_like(sums)
                own = pieces[0][0, back, 0].astype(jnp.float32) * SCALE
                paired = q_rows[...].astype(jnp.float32).reshape(SUB, ROWS, HEAD) * own[None]
                shift[...] = jnp.dot(
                    paired.reshape(SUB * ROWS, HEAD).astype(jnp.bfloat16),
                    jnp.ones((HEAD, LANES), jnp.bfloat16),
                    preferred_element_type=jnp.float32,
                )
            else:
                sums[...] = sums_in[s]
                shift[...] = shift_in[s]

        def weighed(scores, top):
            parts = [scores[:, i * LANES:(i + 1) * LANES] * SCALE - top for i in range(SIDE)]
            weights = jnp.concatenate([jnp.exp2(p).astype(jnp.bfloat16) for p in parts], axis=1)
            high = jnp.maximum(jnp.maximum(parts[0], parts[1]), jnp.maximum(parts[2], parts[3]))
            return jnp.dot(weights, values[...], preferred_element_type=jnp.float32), high

        def quick(chunk, carry):
            fetch(chunk)

            def update(scores):
                added, high = weighed(scores, shift[...])
                sums[...] += added
                highest[...] = jnp.maximum(highest[...], jnp.max(high.reshape(ROWS, SUB, LANES), axis=0))

            whole = (block_of(chunk * SIDE) < query_block) & (block_of(chunk * SIDE + SIDE - 1) * ROWS >= last_start)
            pl.when(whole)(lambda: update(scored()))
            pl.when(jnp.logical_not(whole))(lambda: update(masked(scored(), chunk)))
            return carry

        def careful(chunk, carry):
            fetch(chunk)
            scores = masked(scored(), chunk)
            before = shift[...]
            fresh = jnp.maximum(before, SCALE * jnp.max(scores, axis=1, keepdims=True))
            shrink = jnp.exp2(before - fresh)
            shift[...] = fresh
            added = weighed(scores, fresh)[0]
            sums[...] = sums[...] * jnp.concatenate([shrink, shrink], axis=1) + added
            return carry

        begin()
        highest[...] = jnp.full_like(highest, NEG)
        lax.fori_loop(0, chunks, quick, 0)

        @pl.when(jnp.logical_not(jnp.max(highest[...]) < SAFE))
        def _():
            begin()
            lax.fori_loop(0, chunks, careful, 0)

        if not near:
            for i in range(count):
                @pl.when(s == i)
                def _():
                    for g in range(SUB):
                        rows = slice(g * ROWS, (g + 1) * ROWS)
                        o_refs[i][:, g * HEAD:(g + 1) * HEAD] = (
                            sums[rows, :HEAD] / sums[rows, HEAD:]
                        ).astype(jnp.bfloat16)
        return unused

    lax.fori_loop(0, count, query, 0)


def joined(place_ref, base_ref, parts, store):
    rows, width = base_ref.shape
    cols = width // SIDE
    for r, part in enumerate(parts):
        start = pl.multiple_of(((place_ref[0] + r) & (SIDE - 1)) * cols, cols)
        heads = part[...]
        stream = base_ref[:, pl.ds(start, cols)] + heads.astype(jnp.float32)
        store(pl.ds(start, cols), heads, stream.astype(jnp.bfloat16))


def squares_kernel(place_ref, base_ref, p0, p1, p2, p3, squares_ref):
    squares_ref[...] = jnp.zeros_like(squares_ref)

    def store(cols, heads, stream):
        wide = stream.astype(jnp.float32)
        squares_ref[...] += jnp.sum(wide * wide, axis=1, keepdims=True)

    joined(place_ref, base_ref, (p0, p1, p2, p3), store)


def stream_kernel(place_ref, base_ref, p0, p1, p2, p3, squares_ref, stream_ref, attended_ref):
    def store(cols, heads, stream):
        attended_ref[:, cols] = heads
        stream_ref[:, cols] = stream

    joined(place_ref, base_ref, (p0, p1, p2, p3), store)


def normed_kernel(width, stream_ref, gain_ref, own_ref, other_ref, normed_ref):
    factor = lax.rsqrt((own_ref[...] + other_ref[...]) / (2 * width) + 1e-06)
    normed_ref[...] = (stream_ref[...].astype(jnp.float32) * factor * gain_ref[...]).astype(jnp.bfloat16)


def apart(place, keys_values):
    return pl.pallas_call(
        apart_kernel,
        in_specs=[SMEM, VMEM],
        out_specs=[VMEM] * SIDE,
        out_shape=[jax.ShapeDtypeStruct((2, ROWS, HEAD), jnp.bfloat16)] * SIDE,
        compiler_params=PARAMS,
        name="apart",
    )(place, keys_values)


def mode_states(x, halo, taps, rates, weights, before):
    width = rates.shape[1]
    steps = width // GROUP // 2
    skip = steps if before else 0
    by_modes = pl.BlockSpec((MODES, GROUP), lambda i: (0, i + skip))
    by_state = pl.BlockSpec((MODES, SUB, LANES), lambda i: (0, i + skip, 0))
    by_time = pl.BlockSpec((ROWS * SUB, LANES), lambda i: (i + skip, 0))
    turned = jax.ShapeDtypeStruct((ROWS * width // LANES, LANES), jnp.float32)
    states = jax.ShapeDtypeStruct((MODES, width // LANES, LANES), jnp.float32)
    count = len(before)

    def kernel(*refs):
        states_kernel(*refs[:5], *refs[5 + count:])

    return pl.pallas_call(
        kernel,
        grid=(steps,),
        in_specs=[
            pl.BlockSpec((3, ROWS, GROUP), lambda i: (0, 0, i + skip)),
            pl.BlockSpec((3, SUB, GROUP), lambda i: (0, 0, i + skip)),
            pl.BlockSpec((3, SHORT, GROUP), lambda i: (0, 0, i + skip)),
            by_modes,
            by_modes,
        ] + [ANY] * count,
        input_output_aliases={5 + i: i for i in range(count)},
        out_specs=[by_time, by_time, by_state, by_state, by_state],
        out_shape=[turned, turned, states, states, states],
        scratch_shapes=[
            pltpu.VMEM((3, (SUB + ROWS) * SUB, LANES), jnp.float32),
            pltpu.VMEM((3, SUB * SUB, LANES), jnp.float32),
            pltpu.VMEM((2, MODES * SUB, LANES), jnp.float32),
        ],
        compiler_params=PARAMS,
        cost_estimate=pl.CostEstimate(flops=30_000_000, bytes_accessed=10_000_000, transcendentals=0),
        name="mode_states",
    )(x, halo, taps, rates, weights, *before)


def mixed(state, rate, weight, gated, first, residual, after):
    rows, width = residual.shape
    modes = pl.BlockSpec((MODES, SUB, LANES), lambda i: (0, i, 0))
    by_time = pl.BlockSpec((ROWS * SUB, LANES), lambda i: (i, 0))
    by_rows = pl.BlockSpec((ROWS, GROUP), lambda i: (0, i))
    return pl.pallas_call(
        mixed_kernel,
        grid=(width // GROUP,),
        in_specs=[modes, modes, modes, by_time, by_time, by_rows, ANY, ANY],
        out_specs=by_rows,
        out_shape=jax.ShapeDtypeStruct((rows, width), jnp.float32),
        scratch_shapes=[
            pltpu.VMEM((MODES, SUB, LANES), jnp.float32),
            pltpu.VMEM((ROWS * SUB, LANES), jnp.float32),
        ],
        compiler_params=PARAMS,
        cost_estimate=pl.CostEstimate(flops=40_000_000, bytes_accessed=20_000_000, transcendentals=0),
        name="mixed",
    )(state, rate, weight, gated, first, residual, *after)


def level(span, which, place, rate, own, others, after):
    state = jax.ShapeDtypeStruct(rate.shape, jnp.float32)
    return pl.pallas_call(
        lambda *refs: level_kernel(span, which, *refs),
        in_specs=[SMEM] + [VMEM] * 5 + [ANY],
        out_specs=[VMEM, VMEM],
        out_shape=[state, state],
        compiler_params=PARAMS,
        cost_estimate=pl.CostEstimate(flops=1_000_000, bytes_accessed=3_000_000, transcendentals=0),
        name="level",
    )(place, rate, own, *others, after)


def entering(place, rate, before_x, before_z, others, after):
    return pl.pallas_call(
        entering_kernel,
        in_specs=[SMEM] + [VMEM] * 6 + [ANY],
        out_specs=VMEM,
        out_shape=jax.ShapeDtypeStruct(rate.shape, jnp.float32),
        compiler_params=PARAMS,
        cost_estimate=pl.CostEstimate(flops=1_000_000, bytes_accessed=3_000_000, transcendentals=0),
        name="entering",
    )(place, rate, before_x, before_z, *others, after)


def attend_scratch():
    return [
        pltpu.VMEM((SUB * ROWS, HEAD), jnp.bfloat16),
        pltpu.VMEM((CHUNK, HEAD), jnp.bfloat16),
        pltpu.VMEM((CHUNK, 2 * HEAD), jnp.bfloat16),
        pltpu.VMEM((SUB * ROWS, 2 * HEAD), jnp.float32),
        pltpu.VMEM((SUB * ROWS, LANES), jnp.float32),
        pltpu.VMEM((SUB, LANES), jnp.float32),
    ]


def attend_near(backs, place, lengths, asked, row, after):
    count = len(backs)
    return pl.pallas_call(
        lambda *refs: attend_kernel(backs, True, *refs),
        in_specs=[SMEM, SMEM] + [VMEM] * (count + 1) + [ANY, ANY],
        out_specs=[VMEM, VMEM],
        out_shape=[
            jax.ShapeDtypeStruct((count, SUB * ROWS, 2 * HEAD), jnp.float32),
            jax.ShapeDtypeStruct((count, SUB * ROWS, LANES), jnp.float32),
        ],
        scratch_shapes=attend_scratch(),
        compiler_params=PARAMS,
        cost_estimate=pl.CostEstimate(flops=4_000_000_000, bytes_accessed=10_000_000, transcendentals=3_000_000),
        name="attend_near",
    )(place, lengths, *[asked[r] for r in backs], row, *after)


def attend_far(backs, place, lengths, asked, pieces, sums, shift, after):
    count = len(backs)
    out = jax.ShapeDtypeStruct((ROWS, SUB * HEAD), jnp.bfloat16)
    return pl.pallas_call(
        lambda *refs: attend_kernel(backs, False, *refs),
        in_specs=[SMEM, SMEM] + [VMEM] * (count + SIDE + 2) + [ANY, ANY],
        out_specs=[VMEM] * count,
        out_shape=[out] * count,
        scratch_shapes=attend_scratch(),
        compiler_params=PARAMS,
        cost_estimate=pl.CostEstimate(flops=6_000_000_000, bytes_accessed=15_000_000, transcendentals=3_000_000),
        name="attend_far",
    )(place, lengths, *[asked[r] for r in backs], *pieces, sums, shift, *after)


def squared(place, base, parts):
    return pl.pallas_call(
        squares_kernel,
        in_specs=[SMEM] + [VMEM] * (SIDE + 1),
        out_specs=VMEM,
        out_shape=jax.ShapeDtypeStruct((base.shape[0], 1), jnp.float32),
        compiler_params=PARAMS,
        name="squared",
    )(place, base, *parts)


def streamed(place, base, parts, after):
    wide = jax.ShapeDtypeStruct(base.shape, jnp.bfloat16)
    return pl.pallas_call(
        stream_kernel,
        in_specs=[SMEM] + [VMEM] * (SIDE + 1) + [ANY],
        out_specs=[VMEM, VMEM],
        out_shape=[wide, wide],
        compiler_params=PARAMS,
        cost_estimate=pl.CostEstimate(flops=4_000_000, bytes_accessed=9_000_000, transcendentals=0),
        name="streamed",
    )(place, base, *parts, after)


def normalized(stream, gain, own, other):
    rows, width = stream.shape
    block = pl.BlockSpec((rows, width // SIDE), lambda i: (0, i))
    whole = pl.BlockSpec(own.shape, lambda i: (0, 0))
    return pl.pallas_call(
        lambda *refs: normed_kernel(width, *refs),
        grid=(SIDE,),
        in_specs=[block, pl.BlockSpec((1, width // SIDE), lambda i: (0, i)), whole, whole],
        out_specs=block,
        out_shape=jax.ShapeDtypeStruct(stream.shape, jnp.bfloat16),
        compiler_params=PARAMS,
        name="normalized",
    )(stream, gain, own, other)


def local(streams, short_taps, rates, residues, residual, gain, queries, keys_values, lengths):
    width = residual.shape[1]
    head_cols = width // SIDE
    y, z, x = (lax.axis_index(a) for a in ("y", "z", "x"))
    place = jnp.stack([y, z, x, lax.axis_index("tp")])

    by_stream = streams.transpose(1, 0, 2)
    route = [(i, i + 1) for i in range(SIDE**3 - 1)]
    halo = lax.ppermute(by_stream[:, ROWS - SUB:], ("y", "z", "x"), route)
    near = [turn(value, "y", r) for r, value in enumerate(apart(place, keys_values))]
    asked = [
        turn(lax.dynamic_slice_in_dim(queries, ((y + r) & (SIDE - 1)) * head_cols, head_cols, 1), "y", r)
        for r in range(SIDE)
    ]
    part, halo = lax.optimization_barrier((jnp.stack(near), halo))
    weights = residues * jnp.sqrt(-jnp.expm1(-2.0 * rates))
    row = jnp.stack([turn_cores(part, k, "xz") for k in range(SIDE)])
    taps = short_taps.transpose(1, 0, 2)
    partial = mode_states(by_stream, halo, taps, rates, weights, ())
    row, asked[1], asked[3], end = lax.optimization_barrier((row, asked[1], asked[3], partial[2]))
    halo, _ = lax.optimization_barrier((halo, row))
    left, right = turn_cores(row, 1, "zx"), turn_cores(row, SIDE - 1, "zx")
    first, gated, end, rate, weight = mode_states(
        by_stream, halo, taps, rates, weights, (*partial[:2], end, *partial[3:])
    )

    def others(value, axis):
        sent = value.astype(jnp.bfloat16)
        return [turn(sent, axis, k) for k in range(1, SIDE)]

    def far(backs, sums, *after):
        return attend_far(backs, place, lengths, asked, pieces, *sums, after)

    end, asked[2] = lax.optimization_barrier((end, asked[2]))
    others_x = others(end, "x")
    half = SIDE // 2
    pieces = [left, turn_cores(left[:half], 1, "zx"), turn_cores(right[half:], SIDE - 1, "zx"), right]
    odd = attend_near((1, 3), place, lengths, asked, row, (left, right))
    before_x, total = level(ROWS, 2, place, rate, end, others_x, odd[1])
    others_z = others(total, "z")
    even = attend_near((2, 0), place, lengths, asked, row, (total, odd[1]))
    before_z, total = level(ROWS * SIDE, 1, place, rate, total, others_z, even[1])
    others_y = others(total, "y")
    parts = [None] * SIDE
    parts[1], parts[3] = far((1, 3), odd, total, total)
    state = entering(place, rate, before_x, before_z, others_y, parts[1])
    parts[2], parts[0] = far((2, 0), even, state, parts[3])
    for r in (1, 3):
        parts[r] = turn(parts[r], "y", SIDE - r)
    base = mixed(state, rate, weight, gated, first, residual, (parts[1], parts[3]))
    parts[0], parts[2] = lax.optimization_barrier((parts[0], parts[2]))
    parts[2] = turn(parts[2], "y", SIDE - 2)
    own = squared(place, base, parts)
    other = lax.ppermute(own, "tp", [(0, 1), (1, 0)])
    stream, attended = streamed(place, base, parts, own)
    normed = normalized(stream, gain[None], own, other)
    return (stream, normed, attended)


def solution(mesh):
    split = Mesh(mesh.devices.reshape(SIDE, SIDE, SIDE, 2), MESH)
    ctx = MESH[:3]
    in_specs = (
        P(ctx, None, "tp"),
        P(None, None, "tp"),
        P(None, "tp"),
        P(None, "tp"),
        P(ctx, "tp"),
        P("tp"),
        P(ctx, "tp"),
        P(ctx, None, "tp"),
        P(),
    )
    out_specs = (P(ctx, "tp"), P(ctx, "tp"), P(ctx, "tp"))
    return jax.shard_map(local, mesh=split, in_specs=in_specs, out_specs=out_specs, check_vma=False)
```
